32 devices in a mesh: tiles: 8 (over z, core), chan: 4 (over y, x).
Axes of the slice: x: 2, y: 2, z: 4, core: 2. Of those that a mesh axis runs over, the one named last changes fastest.
Arguments:
- atmos_state: bfloat16 [64, 192, 256], P('tiles', 'chan'), may hold values from -6 to 6
- ocean_state: bfloat16 [64, 128, 256], P('tiles', 'chan'), may hold values from -6 to 6
- atmos_weight: bfloat16 [9, 192, 192], P(None, 'chan'), may hold values from -0.15625 to 0.15625
- ocean_weight: bfloat16 [9, 128, 128], P(None, 'chan'), may hold values from -0.1875 to 0.1875
- couple_weight: bfloat16 [128, 192], P('chan'), may hold values from -0.4375 to 0.4375
- sea_mask: int32 [64], replicated, may hold values from 0 to 1, as said below
- neighbours: int32 [64, 4], replicated, may hold values from 0 to 63, as said below
- rotations: int32 [64, 4], replicated, may hold values from 0 to 7
Outputs:
- atmos_next: bfloat16 [64, 192, 256], P('tiles', 'chan')
- ocean_next: bfloat16 [48, 128, 256], P('tiles', 'chan')
The draws below stay inside these ranges and needn't reach their ends.
Inputs may be any that keep to these rules, and one draw needn't show every extreme that they name: `sea_mask`: exactly 48 of the 64 entries are 1; the tiles of blocks 2k and 2k + 1 of 8 tiles hold exactly 12 sea tiles together, and each such block holds between 4 and 8. neighbours[t, s] lies in the block of 8 tiles that holds t, or in the block just before or just after it, cyclically over the 8 blocks.
All inputs are finite; a program needn't handle non-finite values.
Results may differ from the reference program's by a relative error of at most 0.0034.
Values may be sent and summed in bfloat16 or wider, within the bound.
A program may use at most 64 MiB of HBM per device.

```python
import jax
import jax.numpy as jnp
from jax import lax

A_CH = 192
O_CH = 128
SIDE = 16
TPD = 8
OPD = 6
TILES = 64
OCEAN_TILES = 48
N_TILES = 8


def draw_sea_mask(key, part):
    key_shift = jax.random.fold_in(key, 11)
    key_order = jax.random.fold_in(key, 12)
    blocks = TILES // TPD
    pairs = blocks // 2
    shifts = jax.random.randint(key_shift, (pairs,), -(TPD // 4), TPD // 4 + 1).astype(jnp.int32)
    counts = jnp.stack([OPD + shifts, OPD - shifts], axis=1).reshape(blocks).astype(jnp.int32)
    tile_ids = jnp.arange(TILES, dtype=jnp.int32)
    block_ids = tile_ids // TPD
    scores = block_ids * TILES + jax.random.permutation(key_order, TILES).astype(jnp.int32)
    order = jnp.argsort(scores, stable=True).astype(jnp.int32)
    places = jnp.zeros((TILES,), jnp.int32).at[order].set(tile_ids)
    within = places - block_ids * TPD
    return (within < counts[block_ids]).astype(jnp.int32)


def draw_neighbours(key, part):
    key_step = jax.random.fold_in(key, 21)
    key_pick = jax.random.fold_in(key, 22)
    blocks = TILES // TPD
    tile_ids = jnp.arange(TILES, dtype=jnp.int32)
    step_block = jax.random.randint(key_step, (TILES, 4), -1, 2).astype(jnp.int32)
    target_block = ((tile_ids // TPD)[:, None] + step_block) % blocks
    return (target_block * TPD + jax.random.randint(key_pick, (TILES, 4), 0, TPD)).astype(jnp.int32)


def set_ends(values, rng, low, top_value):
    shape = values.shape
    spot = [jax.random.randint(jax.random.fold_in(rng, axis), (), 0, shape[axis]) for axis in range(len(shape))]
    values = values.at[tuple(spot)].set(low)
    longest = shape.index(max(shape))
    spot[longest] = (spot[longest] + 1) % shape[longest]
    return values.at[tuple(spot)].set(top_value)


def block_levels(stream_key, shape, shards, smallest, top_value):
    gain = 1.0
    for dim, shards_of in shards:
        draws = jax.random.uniform(jax.random.fold_in(jax.random.fold_in(stream_key, 6), dim), (shards_of,), jnp.float32, smallest / len(shards), top_value / len(shards))
        gain = gain * jnp.repeat(jnp.exp(draws), shape[dim] // shards_of).reshape((-1,) + (1,) * (len(shape) - 1 - dim))
    return gain


def gaussian(key, dims, deviation, limit, pieces=(), held_as=jnp.bfloat16):
    drawn = jax.random.normal(key, dims, jnp.float32) * deviation
    if len(pieces) > 0:
        drawn = block_levels(key, dims, pieces, -0.22, 0.18) * drawn
    return jnp.clip(drawn, min=-limit, max=limit).astype(held_as)


def setup_inputs(seed: int = 0) -> dict:
    arg_keys = jax.random.split(jax.random.key(seed), 9)
    return {
        "atmos_state": gaussian(arg_keys[0], (TILES, A_CH, SIDE * SIDE), 1.0, 6.0, ((0, 8), (1, 4))),
        "ocean_state": gaussian(arg_keys[1], (TILES, O_CH, SIDE * SIDE), 1.0, 6.0, ((0, 8), (1, 4))),
        "atmos_weight": gaussian(arg_keys[2], (9, A_CH, A_CH), (9 * A_CH) ** -0.5, 0.15625, ((1, 4),)),
        "ocean_weight": gaussian(arg_keys[3], (9, O_CH, O_CH), (9 * O_CH) ** -0.5, 0.1875, ((1, 4),)),
        "couple_weight": gaussian(arg_keys[4], (O_CH, A_CH), A_CH ** -0.5, 0.4375, ((0, 4),)),
        "sea_mask": draw_sea_mask(jax.random.fold_in(arg_keys[8], 71), 0),
        "neighbours": draw_neighbours(jax.random.fold_in(arg_keys[8], 71), 0),
        "rotations": set_ends(jax.random.randint(arg_keys[7], (TILES, 4), 0, 8), jax.random.fold_in(arg_keys[7], 1), 0, 7).astype(jnp.int32),
    }


def edge_set(tile_field):
    tile_count, chan_count = tile_field.shape[0], tile_field.shape[1]
    tile_grid = tile_field.reshape(tile_count, chan_count, SIDE, SIDE)
    return jnp.stack([tile_grid[:, :, 0, :], tile_grid[:, :, :, SIDE - 1], tile_grid[:, :, SIDE - 1, :], tile_grid[:, :, :, 0]], axis=2)


def pick_rims(edge_strips, adjacent, turn_codes):
    picked = edge_strips[adjacent]
    side_index = (turn_codes % 4).astype(jnp.int32)
    chosen = picked[:, :, :, 0, :]
    for edge_id in range(1, 4):
        chosen = jnp.where((side_index == edge_id)[:, :, None, None], picked[:, :, :, edge_id, :], chosen)
    return jnp.where((turn_codes >= 4)[:, :, None, None], chosen[..., ::-1], chosen)


def pad_tile(tile_field, rim_cells):
    tile_count, chan_count = tile_field.shape[0], tile_field.shape[1]
    tile_grid = tile_field.reshape(tile_count, chan_count, SIDE, SIDE)
    upper_row = jnp.pad(rim_cells[:, 0], ((0, 0), (0, 0), (1, 1)))[:, :, None, :]
    bottom = jnp.pad(rim_cells[:, 2], ((0, 0), (0, 0), (1, 1)))[:, :, None, :]
    middle = jnp.concatenate([rim_cells[:, 3][:, :, :, None], tile_grid, rim_cells[:, 1][:, :, :, None]], axis=3)
    assembled = jnp.concatenate([upper_row, middle, bottom], axis=2).reshape(tile_count, chan_count, (SIDE + 2) * (SIDE + 2))
    return jnp.pad(assembled, ((0, 0), (0, 0), (0, 2)))


def conv_sum(padded, weight):
    row_width = SIDE + 2
    out_span = SIDE * row_width
    accum = jnp.zeros((padded.shape[0], weight.shape[1], out_span), jnp.float32)
    for tap_index in range(9):
        offset = (tap_index // 3) * row_width + tap_index % 3
        accum = accum + jnp.einsum("oc,bcp->bop", weight[tap_index].astype(jnp.float32), padded[:, :, offset:offset + out_span].astype(jnp.float32))
    return accum


def trim_columns(accum):
    tile_count, chan_count = accum.shape[0], accum.shape[1]
    return accum.reshape(tile_count, chan_count, SIDE, SIDE + 2)[:, :, :, :SIDE].reshape(tile_count, chan_count, SIDE * SIDE)


def reference(atmos_state, ocean_state, atmos_weight, ocean_weight, couple_weight, sea_mask, neighbours, rotations):
    sea_field = ocean_state * sea_mask.astype(ocean_state.dtype)[:, None, None]
    atmos_edges = edge_set(atmos_state)
    sea_edges = edge_set(sea_field)

    def atmos_block(block_index):
        first_tile = block_index * TPD
        tile_field = lax.dynamic_slice_in_dim(atmos_state, first_tile, TPD, 0)
        adjacent = lax.dynamic_slice_in_dim(neighbours, first_tile, TPD, 0)
        turn_codes = lax.dynamic_slice_in_dim(rotations, first_tile, TPD, 0)
        accum = conv_sum(pad_tile(tile_field, pick_rims(atmos_edges, adjacent, turn_codes)), atmos_weight)
        return (tile_field.astype(jnp.float32) + jax.nn.gelu(trim_columns(accum), approximate=True)).astype(jnp.bfloat16)

    atmos_next = lax.map(atmos_block, jnp.arange(TILES // TPD, dtype=jnp.int32)).reshape(atmos_state.shape)

    sea_flags = sea_mask.astype(jnp.int32)
    sea_rank = (jnp.cumsum(sea_flags) - 1).astype(jnp.int32)
    rank_spots = jnp.where(sea_flags == 1, sea_rank, OCEAN_TILES).astype(jnp.int32)
    tile_of_rank = jnp.zeros((OCEAN_TILES,), jnp.int32).at[rank_spots].set(jnp.arange(TILES, dtype=jnp.int32), mode="drop")
    row_ids = jnp.arange(OCEAN_TILES, dtype=jnp.int32)
    row_ranks = (row_ids // (2 * OPD)) * (2 * OPD) + 2 * (row_ids % OPD) + (row_ids // OPD) % 2
    chosen_tiles = tile_of_rank[row_ranks.astype(jnp.int32)]

    def ocean_block(block_index):
        tiles_now = lax.dynamic_slice_in_dim(chosen_tiles, block_index * OPD, OPD, 0)
        own_state = ocean_state[tiles_now]
        rim_cells = pick_rims(sea_edges, neighbours[tiles_now], rotations[tiles_now])
        mixed = trim_columns(conv_sum(pad_tile(own_state, rim_cells), ocean_weight))
        forcing = atmos_next[tiles_now]
        mixed = mixed + jnp.einsum("oc,bcp->bop", couple_weight.astype(jnp.float32), forcing.astype(jnp.float32))
        return (own_state.astype(jnp.float32) + jax.nn.gelu(mixed, approximate=True)).astype(jnp.bfloat16)

    ocean_next = lax.map(ocean_block, jnp.arange(N_TILES, dtype=jnp.int32)).reshape(OCEAN_TILES, O_CH, SIDE * SIDE)
    return (atmos_next, ocean_next)
```

```python
import functools

import jax
import jax.numpy as jnp
import numpy as np
from jax import lax
from jax.experimental import pallas as pl
from jax.experimental.pallas import tpu as pltpu
from jax.sharding import PartitionSpec as P

SIDE = 16


def padded_2(cells, sides, width):
    for axis, dim in sides:
        count = lax.axis_size(axis)
        head = lax.slice_in_dim(cells, 0, width, axis=dim)
        tail = lax.slice_in_dim(cells, cells.shape[dim] - width, cells.shape[dim], axis=dim)
        cells = jnp.concatenate(
            [
                lax.ppermute(tail, axis, [(i, (i + 1) % count) for i in range(count)]),
                cells,
                lax.ppermute(head, axis, [((i + 1) % count, i) for i in range(count)]),
            ],
            axis=dim,
        )
    return cells


def partner(value, axis, distance):
    mask = 2**distance
    pairs = [(source, source ^ mask) for source in range(lax.axis_size(axis))]
    return lax.ppermute(value, axis, pairs)


def edge_set(tile_field):
    tile_count, chan_count = (tile_field.shape[0], tile_field.shape[1])
    tile_grid = tile_field.reshape(tile_count, chan_count, SIDE, SIDE)
    return jnp.stack(
        [
            tile_grid[:, :, 0, :],
            tile_grid[:, :, :, SIDE - 1],
            tile_grid[:, :, SIDE - 1, :],
            tile_grid[:, :, :, 0],
        ],
        axis=2,
    )


def pick_rims(edge_strips, adjacent, turn_codes):
    picked = edge_strips[adjacent]
    side_index = turn_codes % 4
    chosen = picked[:, :, :, 0, :]
    for edge_id in range(1, 4):
        chosen = jnp.where(
            (side_index == edge_id)[:, :, None, None], picked[:, :, :, edge_id, :], chosen
        )
    return jnp.where((turn_codes >= 4)[:, :, None, None], chosen[..., ::-1], chosen)


def pad_tile(tile_field, rim_cells):
    tile_count, chan_count = (tile_field.shape[0], tile_field.shape[1])
    tile_grid = tile_field.reshape(tile_count, chan_count, SIDE, SIDE)
    upper_row = jnp.pad(rim_cells[:, 0], ((0, 0), (0, 0), (1, 1)))[:, :, None, :]
    bottom = jnp.pad(rim_cells[:, 2], ((0, 0), (0, 0), (1, 1)))[:, :, None, :]
    middle = jnp.concatenate(
        [rim_cells[:, 3][:, :, :, None], tile_grid, rim_cells[:, 1][:, :, :, None]], axis=3
    )
    assembled = jnp.concatenate([upper_row, middle, bottom], axis=2).reshape(
        tile_count, chan_count, (SIDE + 2) * (SIDE + 2)
    )
    return jnp.pad(assembled, ((0, 0), (0, 0), (0, 2)))


def trim_columns(accum):
    tile_count, chan_count = (accum.shape[0], accum.shape[1])
    return accum.reshape(tile_count, chan_count, SIDE, SIDE + 2)[:, :, :, :SIDE].reshape(
        tile_count, chan_count, SIDE * SIDE
    )


def conv_step(weight, accum, piece):
    row_width = SIDE + 2
    out_span = SIDE * row_width
    for tap_index in range(9):
        offset = tap_index // 3 * row_width + tap_index % 3
        accum = accum + jnp.einsum(
            "oc,bcp->bop",
            weight[tap_index],
            piece[:, :, offset : offset + out_span],
            preferred_element_type=jnp.float32,
        )
    return accum


def ocean_layer(padded, forcing, own_state, ocean_weight, couple_weight):
    tile_count = padded.shape[0]
    out_chans = ocean_weight.shape[1]
    conv_start = jnp.zeros((tile_count, out_chans, SIDE * (SIDE + 2)), jnp.float32)
    conv_accum = conv_step(
        ocean_weight, conv_start, lax.all_gather(padded, "chan", axis=1, tiled=True)
    )
    couple_accum = jnp.einsum(
        "oc,bcp->bop",
        couple_weight,
        lax.all_gather(forcing, "chan", axis=1, tiled=True),
        preferred_element_type=jnp.float32,
    )
    mixed = trim_columns(conv_accum) + couple_accum
    return (own_state.astype(jnp.float32) + jax.nn.gelu(mixed, approximate=True)).astype(
        jnp.bfloat16
    )


def local(
    atmos_state,
    ocean_state,
    atmos_weight,
    ocean_weight,
    couple_weight,
    sea_mask,
    neighbours,
    rotations,
):
    per_dev = atmos_state.shape[0]
    atmos_local = atmos_state.shape[1]
    ocean_local = ocean_state.shape[1]
    groups = lax.axis_size("tiles")
    tile_group = lax.axis_index("tiles")
    first_tile = tile_group * per_dev
    sea_here = lax.dynamic_slice_in_dim(sea_mask, first_tile, per_dev, 0)
    sea_field = ocean_state * sea_here.astype(jnp.bfloat16)[:, None, None]
    edge_strips = jnp.concatenate([edge_set(atmos_state), edge_set(sea_field)], axis=1)
    widened = padded_2(edge_strips.reshape(per_dev, -1), (("tiles", 0),), per_dev)
    widened = widened.reshape(3 * per_dev, atmos_local + ocean_local, 4, SIDE)
    adjacent = lax.dynamic_slice_in_dim(neighbours, first_tile, per_dev, 0)
    turn_codes = lax.dynamic_slice_in_dim(rotations, first_tile, per_dev, 0)
    local_adjacent = (adjacent // per_dev - tile_group + 1) % groups * per_dev + adjacent % per_dev
    rim_cells = pick_rims(widened, local_adjacent, turn_codes)
    atmos_pad = pad_tile(atmos_state, rim_cells[:, :, :atmos_local])
    atmos_start = jnp.zeros((per_dev, atmos_weight.shape[1], SIDE * (SIDE + 2)), jnp.float32)
    atmos_accum = conv_step(
        atmos_weight, atmos_start, lax.all_gather(atmos_pad, "chan", axis=1, tiled=True)
    )
    atmos_next = (
        atmos_state.astype(jnp.float32) + jax.nn.gelu(trim_columns(atmos_accum), approximate=True)
    ).astype(jnp.bfloat16)
    per_owner = per_dev * 3 // 4
    ocean_total = per_owner * groups
    counts = jnp.sum(sea_mask.reshape(groups, per_dev), axis=1)
    starts = jnp.cumsum(counts) - counts
    sea_rank = jnp.cumsum(sea_mask) - 1
    rank_spots = jnp.where(sea_mask == 1, sea_rank, ocean_total)
    tile_of_rank = (
        jnp.zeros((ocean_total,), jnp.int32)
        .at[rank_spots]
        .set(jnp.arange(sea_mask.shape[0], dtype=jnp.int32), mode="drop")
    )
    my_first = starts[tile_group]
    my_last = my_first + counts[tile_group]
    parity = tile_group % 2
    pair_base = tile_group // 2 * 2 * per_owner
    slot_ids = jnp.arange(per_owner, dtype=jnp.int32)
    ranks_send = pair_base + 2 * slot_ids + (1 - parity)
    ranks_own = pair_base + 2 * slot_ids + parity
    send_tile = jnp.clip(tile_of_rank[ranks_send] - first_tile, 0, per_dev - 1)
    own_tile = jnp.clip(tile_of_rank[ranks_own] - first_tile, 0, per_dev - 1)
    from_here = (ranks_own >= my_first) & (ranks_own < my_last)
    block_width = (ocean_local + atmos_local) * SIDE * SIDE
    sea_block = jnp.concatenate([ocean_state, atmos_next], axis=1).reshape(per_dev, block_width)
    rim_flat = rim_cells[:, :, atmos_local:].reshape(per_dev, -1)
    packed = jnp.concatenate([sea_block, rim_flat], axis=1)
    received = partner(packed[send_tile], "tiles", 0)
    own_packed = jnp.where(from_here[:, None], packed[own_tile], received)
    own_block = own_packed[:, :block_width].reshape(
        per_owner, ocean_local + atmos_local, SIDE * SIDE
    )
    own_rims = own_packed[:, block_width:].reshape(per_owner, 4, ocean_local, SIDE)
    own_state = own_block[:, :ocean_local]
    ocean_next = ocean_layer(
        pad_tile(own_state, own_rims),
        own_block[:, ocean_local:],
        own_state,
        ocean_weight,
        couple_weight,
    )
    return (atmos_next, ocean_next)


MESH = pl.DeviceIdType.MESH
PIX = SIDE * SIDE
BF = jnp.bfloat16
F32 = jnp.float32


def edge_matrix():
    out = np.zeros((2, PIX, 128), np.float32)
    for half in range(2):
        for q in range(SIDE):
            pixels = (q, q * SIDE + SIDE - 1, (SIDE - 1) * SIDE + q, q * SIDE)
            for edge, pixel in enumerate(pixels):
                out[half, pixel, half * 64 + edge * SIDE + q] = 1
    return out


def shift_matrix():
    out = np.zeros((9, PIX + 128, PIX), np.float32)
    for tap in range(9):
        for i in range(SIDE):
            for j in range(SIDE):
                row, col = i + tap // 3 - 1, j + tap % 3 - 1
                in_row, in_col = 0 <= row < SIDE, 0 <= col < SIDE
                if in_row and in_col:
                    out[tap, row * SIDE + col, i * SIDE + j] = 1
                elif in_row or in_col:
                    if in_col:
                        place = (0 if row < 0 else 2) * SIDE + col
                    else:
                        place = (3 if col < 0 else 1) * SIDE + row
                    for half in range(2):
                        out[tap, PIX + half * 64 + place, i * SIDE + j] = 1
    return out


def gelu(v):
    return 0.5 * v * (1.0 + jnp.tanh(np.float32(np.sqrt(2.0 / np.pi)) * (v + 0.044715 * (v * v * v))))


def dot(x, y):
    return jnp.dot(x, y, preferred_element_type=F32)


def owner_kernel(
    groups, nchan, at_hbm, oc_hbm, wa_hbm, wo_hbm, wc_hbm, mask_s, nbr_s, rot_s, ev_hbm, sh_hbm,
    outa, outo,
    at_v, oc_v, ev, sh, xx, ew, rl, rg, sel, wa, wo, wc, xs, an, on, og,
    loc, ssem, rsem,
):
    per_dev, ach, _ = at_hbm.shape
    och = oc_hbm.shape[1]
    atot = ach * nchan
    tp = per_dev // nchan
    rows = ach + och
    b = lax.axis_index("tiles")
    c = lax.axis_index("chan")
    par = lax.rem(b, 2)
    sib = b + 1 - 2 * par
    nxt = lax.rem(b + 1, groups)
    prv = lax.rem(b + groups - 1, groups)
    other = jnp.where(par == 0, prv, nxt)
    half_o = och // 2

    bar = pltpu.get_barrier_semaphore()
    for d in range(nchan):
        peer = lax.rem(c + d, nchan)
        if d:
            pl.semaphore_signal(bar, inc=1, device_id=(b, peer), device_id_type=MESH)
        pl.semaphore_signal(bar, inc=1, device_id=(sib, peer), device_id_type=MESH)
    pl.semaphore_signal(bar, inc=1, device_id=(other, c), device_id_type=MESH)

    def arow(i):
        return pl.ds(pl.multiple_of(i * ach, 16), ach)

    def orow(i):
        return pl.ds(pl.multiple_of(i * och, 16), och)

    def xorow(i):
        return pl.ds(pl.multiple_of(atot + i * och, 16), och)

    def ohalf(i, k):
        return pl.ds(pl.multiple_of(i * och + k * half_o, 16), half_o)

    own = pl.ds(c * tp, tp)
    locals_ = [
        (at_hbm, at_v),
        (oc_hbm, oc_v),
        (ev_hbm, ev),
        (at_hbm.at[own], xx.at[:, arow(c), :]),
        (oc_hbm.at[own], xx.at[:, xorow(c), :]),
        (sh_hbm, sh),
        (wa_hbm, wa.at[:, arow(c), :]),
        (wo_hbm, wo.at[:, orow(c), :]),
        (wc_hbm, wc.at[orow(c), :]),
    ]
    lcopies = [pltpu.make_async_copy(s, t, loc.at[i]) for i, (s, t) in enumerate(locals_)]
    for cp in lcopies:
        cp.start()
    for cp in lcopies[:3]:
        cp.wait()

    first = b * per_dev
    lane128 = lax.broadcasted_iota(jnp.int32, (1, 128), 1)
    for u in range(per_dev // 2):
        at_e = dot(at_v[2 * u], ev[0]) + dot(at_v[2 * u + 1], ev[1])
        oc_e = dot(oc_v[2 * u], ev[0]) + dot(oc_v[2 * u + 1], ev[1])
        keep = jnp.where(lane128 < 64, mask_s[first + 2 * u], mask_s[first + 2 * u + 1])
        ew[1, :ach, u * 128 : u * 128 + 128] = at_e.astype(BF)
        ew[1, ach:, u * 128 : u * 128 + 128] = jnp.where(keep > 0, oc_e, 0.0).astype(BF)

    counter = [0]

    def remote(src, dst, dev):
        i = counter[0]
        counter[0] += 1
        return pltpu.make_async_remote_copy(
            src_ref=src, dst_ref=dst, send_sem=ssem.at[i], recv_sem=rsem.at[i],
            device_id=dev, device_id_type=MESH,
        )

    pl.semaphore_wait(bar, 2 * nchan)
    edges = [remote(ew.at[1], ew.at[0], (nxt, c)), remote(ew.at[1], ew.at[2], (prv, c))]
    for cp in edges:
        cp.start()
    states, weights = [], []
    for d in range(1, nchan):
        peer = lax.rem(c + d, nchan)
        theirs = pl.ds(peer * tp, tp)
        states += [
            remote(at_hbm.at[theirs], xx.at[:, arow(c), :], (b, peer)),
            remote(oc_hbm.at[theirs], xx.at[:, xorow(c), :], (b, peer)),
        ]
    for cp in states:
        cp.start()
    for d in range(1, nchan):
        peer = lax.rem(c + d, nchan)
        taps = pl.ds(par * 4, 5)
        hrow = pl.ds(pl.multiple_of(par * half_o, 16), half_o)
        weights += [
            remote(wa_hbm.at[taps], wa.at[taps, arow(c), :], (b, peer)),
            remote(wo_hbm.at[:, hrow, :], wo.at[:, ohalf(c, par), :], (b, peer)),
            remote(wc_hbm.at[hrow], wc.at[ohalf(c, par), :], (b, peer)),
        ]
    for cp in weights:
        cp.start()

    width = per_dev * 64
    lane = lax.broadcasted_iota(jnp.int32, (1, width), 1)
    strip, place = lane // SIDE, lane % SIDE
    src = jnp.zeros((1, width), jnp.int32)
    for t in range(per_dev):
        for s in range(4):
            nb = nbr_s[first + t, s]
            rot = rot_s[first + t, s]
            slot = lax.rem(lax.div(nb, per_dev) - b + 1 + groups, groups)
            base = slot * width + lax.rem(nb, per_dev) * 64 + lax.rem(rot, 4) * SIDE
            back = jnp.where(rot >= 4, SIDE - 1, 0)
            step = jnp.where(rot >= 4, -1, 1)
            src = jnp.where(strip == t * 4 + s, base + back + step * place, src)

    row_ids = lax.broadcasted_iota(jnp.int32, (128, width), 0)

    @pl.loop(0, 3 * width // 128)
    def _(k):
        hit = (row_ids + k * 128) == src
        sel[pl.ds(pl.multiple_of(k * 128, 128), 128), :] = jnp.where(hit, 1.0, 0.0).astype(BF)

    pair_first = (b - par) * per_dev
    nrows = outo.shape[0]
    picks = [jnp.int32(0)] * nrows
    rank = jnp.int32(0)
    for n in range(2 * per_dev):
        sea = mask_s[pair_first + n]
        for i in range(nrows):
            picks[i] = jnp.where((sea == 1) & (rank == 2 * i + par), n, picks[i])
        rank = rank + sea

    for cp in edges:
        cp.wait_recv()
    rim = dot(ew[0], sel[:width]) + dot(ew[1], sel[width : 2 * width]) + dot(ew[2], sel[2 * width :])
    rim = rim.astype(BF)
    for i in range(nchan):
        rl[i] = rim[:, i * 128 : i * 128 + 128]
    rims = []
    for d in range(1, nchan):
        peer = lax.rem(c + d, nchan)
        rims.append(remote(rl.at[peer], rg.at[c], (b, peer)))
    for cp in rims:
        cp.start()
    own_rim = pltpu.make_async_copy(rl.at[c], rg.at[c], loc.at[9])
    own_rim.start()

    for cp in lcopies[3:6]:
        cp.wait()
    for cp in states:
        cp.wait_recv()
    own_rim.wait()
    for cp in rims:
        cp.wait_recv()

    ring = jnp.concatenate(
        [rg[i, :ach] for i in range(nchan)] + [rg[i, ach:] for i in range(nchan)], axis=0
    )
    for j in range(tp):
        mine = jnp.where(lane128 // 64 == j, ring, jnp.zeros_like(ring))
        rl_all = jnp.concatenate([xx[j], mine], axis=1)

        @pl.loop(0, 9)
        def _(tap):
            xs[tap, :, j * PIX : (j + 1) * PIX] = dot(rl_all, sh[tap]).astype(BF)

    forwards = []
    for d in range(1, nchan):
        origin = lax.rem(c + nchan - d, nchan)
        ftaps = pl.ds(par * 5, 4)
        forwards += [
            remote(wa.at[ftaps, arow(origin), :], wa.at[ftaps, arow(origin), :], (sib, c)),
            remote(wo.at[:, ohalf(origin, par), :], wo.at[:, ohalf(origin, par), :], (sib, c)),
            remote(wc.at[ohalf(origin, par), :], wc.at[ohalf(origin, par), :], (sib, c)),
        ]
    for got, fwd in zip(weights, forwards):
        got.wait_recv()
        fwd.start()
    for cp in lcopies[6:]:
        cp.wait()
    for cp in forwards:
        cp.wait_recv()

    dest = pl.ds(c * tp, tp)
    finals = []
    for j in range(tp):
        acc = jnp.zeros((atot, PIX), F32)
        for tap in range(9):
            acc = acc + dot(wa[tap], xs[tap, :atot, j * PIX : (j + 1) * PIX])
        an[j] = (xx[j, :atot].astype(F32) + gelu(acc)).astype(BF)
    for d in range(1, nchan):
        peer = lax.rem(c + d, nchan)
        cp = remote(an.at[:, arow(peer), :], outa.at[dest], (b, peer))
        cp.start()
        finals.append(cp)
    own_a = pltpu.make_async_copy(an.at[:, arow(c), :], outa.at[dest], loc.at[10])
    own_a.start()
    for j in range(tp):
        acc = dot(wc[...], an[j])
        for tap in range(9):
            acc = acc + dot(wo[tap], xs[tap, atot:, j * PIX : (j + 1) * PIX])
        on[j] = (xx[j, atot:].astype(F32) + gelu(acc)).astype(BF)
    odest = pl.ds(par * per_dev + c * tp, tp)
    for d in range(nchan):
        peer = lax.rem(c + d, nchan)
        for block in (b, sib) if d else (sib,):
            cp = remote(on.at[:, orow(peer), :], og.at[odest], (block, peer))
            cp.start()
            finals.append(cp)
    own_o = pltpu.make_async_copy(on.at[:, orow(c), :], og.at[odest], loc.at[11])
    own_o.start()
    own_a.wait()
    own_o.wait()
    for cp in finals:
        cp.wait_recv()
    for i in range(nrows):
        outo[i] = og[picks[i]]
    for cp in edges + states + weights + rims + forwards + finals:
        cp.wait_send()


def local_owner(
    atmos_state, ocean_state, atmos_weight, ocean_weight, couple_weight, sea_mask, neighbours, rotations
):
    groups, nchan = lax.axis_size("tiles"), lax.axis_size("chan")
    per_dev, ach, _ = atmos_state.shape
    och = ocean_state.shape[1]
    atot, otot, tp = ach * nchan, och * nchan, per_dev // nchan
    rows, width = ach + och, per_dev * 64
    copies = 2 + 11 * (nchan - 1) + 10 * (nchan - 1) + nchan + 6
    anyspace = pl.BlockSpec(memory_space=pl.ANY)
    smem = pl.BlockSpec(memory_space=pltpu.SMEM)
    return pl.pallas_call(
        functools.partial(owner_kernel, groups, nchan),
        out_shape=(
            jax.ShapeDtypeStruct(atmos_state.shape, BF),
            jax.ShapeDtypeStruct((per_dev * 3 // 4, och, PIX), BF),
        ),
        in_specs=[anyspace] * 5 + [smem] * 3 + [anyspace] * 2,
        out_specs=(anyspace, pl.BlockSpec(memory_space=pltpu.VMEM)),
        scratch_shapes=[
            pltpu.VMEM((per_dev, ach, PIX), BF),
            pltpu.VMEM((per_dev, och, PIX), BF),
            pltpu.VMEM((2, PIX, 128), BF),
            pltpu.VMEM((9, PIX + 128, PIX), BF),
            pltpu.VMEM((tp, atot + otot, PIX), BF),
            pltpu.VMEM((3, rows, width), BF),
            pltpu.VMEM((nchan, rows, 128), BF),
            pltpu.VMEM((nchan, rows, 128), BF),
            pltpu.VMEM((3 * width, width), BF),
            pltpu.VMEM((9, atot, atot), BF),
            pltpu.VMEM((9, otot, otot), BF),
            pltpu.VMEM((otot, atot), BF),
            pltpu.VMEM((9, atot + otot, tp * PIX), BF),
            pltpu.VMEM((tp, atot, PIX), BF),
            pltpu.VMEM((tp, otot, PIX), BF),
            pltpu.VMEM((2 * per_dev, och, PIX), BF),
            pltpu.SemaphoreType.DMA((12,)),
            pltpu.SemaphoreType.DMA((copies,)),
            pltpu.SemaphoreType.DMA((copies,)),
        ],
        compiler_params=pltpu.CompilerParams(
            collective_id=0, has_side_effects=True, vmem_limit_bytes=40 * 2**20
        ),
        cost_estimate=pl.CostEstimate(flops=2 * 10**9, bytes_accessed=4 * 10**6, transcendentals=170000),
    )(
        atmos_state, ocean_state, atmos_weight, ocean_weight, couple_weight, sea_mask, neighbours, rotations,
        jnp.asarray(edge_matrix(), BF), jnp.asarray(shift_matrix(), BF),
    )


def solution(mesh):
    body = local_owner if mesh.shape["chan"] == 4 else local
    placed = (
        P("tiles", "chan", None),
        P("tiles", "chan", None),
        P(None, "chan", None),
        P(None, "chan", None),
        P("chan", None),
        P(),
        P(),
        P(),
    )
    return jax.shard_map(
        body,
        mesh=mesh,
        in_specs=placed,
        out_specs=(P("tiles", "chan", None), P("tiles", "chan", None)),
        check_vma=False,
    )
```

```python
import functools

import jax
import jax.numpy as jnp
import numpy as np
from jax import lax
from jax.experimental import pallas as pl
from jax.experimental.pallas import tpu as pltpu
from jax.sharding import PartitionSpec as P

SIDE = 16


def padded_2(cells, sides, width):
    for axis, dim in sides:
        count = lax.axis_size(axis)
        head = lax.slice_in_dim(cells, 0, width, axis=dim)
        tail = lax.slice_in_dim(cells, cells.shape[dim] - width, cells.shape[dim], axis=dim)
        cells = jnp.concatenate(
            [
                lax.ppermute(tail, axis, [(i, (i + 1) % count) for i in range(count)]),
                cells,
                lax.ppermute(head, axis, [((i + 1) % count, i) for i in range(count)]),
            ],
            axis=dim,
        )
    return cells


def partner(value, axis, distance):
    mask = 2**distance
    pairs = [(source, source ^ mask) for source in range(lax.axis_size(axis))]
    return lax.ppermute(value, axis, pairs)


def edge_set(tile_field):
    tile_count, chan_count = (tile_field.shape[0], tile_field.shape[1])
    tile_grid = tile_field.reshape(tile_count, chan_count, SIDE, SIDE)
    return jnp.stack(
        [
            tile_grid[:, :, 0, :],
            tile_grid[:, :, :, SIDE - 1],
            tile_grid[:, :, SIDE - 1, :],
            tile_grid[:, :, :, 0],
        ],
        axis=2,
    )


def pick_rims(edge_strips, adjacent, turn_codes):
    picked = edge_strips[adjacent]
    side_index = turn_codes % 4
    chosen = picked[:, :, :, 0, :]
    for edge_id in range(1, 4):
        chosen = jnp.where(
            (side_index == edge_id)[:, :, None, None], picked[:, :, :, edge_id, :], chosen
        )
    return jnp.where((turn_codes >= 4)[:, :, None, None], chosen[..., ::-1], chosen)


def pad_tile(tile_field, rim_cells):
    tile_count, chan_count = (tile_field.shape[0], tile_field.shape[1])
    tile_grid = tile_field.reshape(tile_count, chan_count, SIDE, SIDE)
    upper_row = jnp.pad(rim_cells[:, 0], ((0, 0), (0, 0), (1, 1)))[:, :, None, :]
    bottom = jnp.pad(rim_cells[:, 2], ((0, 0), (0, 0), (1, 1)))[:, :, None, :]
    middle = jnp.concatenate(
        [rim_cells[:, 3][:, :, :, None], tile_grid, rim_cells[:, 1][:, :, :, None]], axis=3
    )
    assembled = jnp.concatenate([upper_row, middle, bottom], axis=2).reshape(
        tile_count, chan_count, (SIDE + 2) * (SIDE + 2)
    )
    return jnp.pad(assembled, ((0, 0), (0, 0), (0, 2)))


def trim_columns(accum):
    tile_count, chan_count = (accum.shape[0], accum.shape[1])
    return accum.reshape(tile_count, chan_count, SIDE, SIDE + 2)[:, :, :, :SIDE].reshape(
        tile_count, chan_count, SIDE * SIDE
    )


def conv_step(weight, accum, piece):
    row_width = SIDE + 2
    out_span = SIDE * row_width
    for tap_index in range(9):
        offset = tap_index // 3 * row_width + tap_index % 3
        accum = accum + jnp.einsum(
            "oc,bcp->bop",
            weight[tap_index],
            piece[:, :, offset : offset + out_span],
            preferred_element_type=jnp.float32,
        )
    return accum


def ocean_layer(padded, forcing, own_state, ocean_weight, couple_weight):
    tile_count = padded.shape[0]
    out_chans = ocean_weight.shape[1]
    conv_start = jnp.zeros((tile_count, out_chans, SIDE * (SIDE + 2)), jnp.float32)
    conv_accum = conv_step(
        ocean_weight, conv_start, lax.all_gather(padded, "chan", axis=1, tiled=True)
    )
    couple_accum = jnp.einsum(
        "oc,bcp->bop",
        couple_weight,
        lax.all_gather(forcing, "chan", axis=1, tiled=True),
        preferred_element_type=jnp.float32,
    )
    mixed = trim_columns(conv_accum) + couple_accum
    return (own_state.astype(jnp.float32) + jax.nn.gelu(mixed, approximate=True)).astype(
        jnp.bfloat16
    )


def local(
    atmos_state,
    ocean_state,
    atmos_weight,
    ocean_weight,
    couple_weight,
    sea_mask,
    neighbours,
    rotations,
):
    per_dev = atmos_state.shape[0]
    atmos_local = atmos_state.shape[1]
    ocean_local = ocean_state.shape[1]
    groups = lax.axis_size("tiles")
    tile_group = lax.axis_index("tiles")
    first_tile = tile_group * per_dev
    sea_here = lax.dynamic_slice_in_dim(sea_mask, first_tile, per_dev, 0)
    sea_field = ocean_state * sea_here.astype(jnp.bfloat16)[:, None, None]
    edge_strips = jnp.concatenate([edge_set(atmos_state), edge_set(sea_field)], axis=1)
    widened = padded_2(edge_strips.reshape(per_dev, -1), (("tiles", 0),), per_dev)
    widened = widened.reshape(3 * per_dev, atmos_local + ocean_local, 4, SIDE)
    adjacent = lax.dynamic_slice_in_dim(neighbours, first_tile, per_dev, 0)
    turn_codes = lax.dynamic_slice_in_dim(rotations, first_tile, per_dev, 0)
    local_adjacent = (adjacent // per_dev - tile_group + 1) % groups * per_dev + adjacent % per_dev
    rim_cells = pick_rims(widened, local_adjacent, turn_codes)
    atmos_pad = pad_tile(atmos_state, rim_cells[:, :, :atmos_local])
    atmos_start = jnp.zeros((per_dev, atmos_weight.shape[1], SIDE * (SIDE + 2)), jnp.float32)
    atmos_accum = conv_step(
        atmos_weight, atmos_start, lax.all_gather(atmos_pad, "chan", axis=1, tiled=True)
    )
    atmos_next = (
        atmos_state.astype(jnp.float32) + jax.nn.gelu(trim_columns(atmos_accum), approximate=True)
    ).astype(jnp.bfloat16)
    per_owner = per_dev * 3 // 4
    ocean_total = per_owner * groups
    counts = jnp.sum(sea_mask.reshape(groups, per_dev), axis=1)
    starts = jnp.cumsum(counts) - counts
    sea_rank = jnp.cumsum(sea_mask) - 1
    rank_spots = jnp.where(sea_mask == 1, sea_rank, ocean_total)
    tile_of_rank = (
        jnp.zeros((ocean_total,), jnp.int32)
        .at[rank_spots]
        .set(jnp.arange(sea_mask.shape[0], dtype=jnp.int32), mode="drop")
    )
    my_first = starts[tile_group]
    my_last = my_first + counts[tile_group]
    parity = tile_group % 2
    pair_base = tile_group // 2 * 2 * per_owner
    slot_ids = jnp.arange(per_owner, dtype=jnp.int32)
    ranks_send = pair_base + 2 * slot_ids + (1 - parity)
    ranks_own = pair_base + 2 * slot_ids + parity
    send_tile = jnp.clip(tile_of_rank[ranks_send] - first_tile, 0, per_dev - 1)
    own_tile = jnp.clip(tile_of_rank[ranks_own] - first_tile, 0, per_dev - 1)
    from_here = (ranks_own >= my_first) & (ranks_own < my_last)
    block_width = (ocean_local + atmos_local) * SIDE * SIDE
    sea_block = jnp.concatenate([ocean_state, atmos_next], axis=1).reshape(per_dev, block_width)
    rim_flat = rim_cells[:, :, atmos_local:].reshape(per_dev, -1)
    packed = jnp.concatenate([sea_block, rim_flat], axis=1)
    received = partner(packed[send_tile], "tiles", 0)
    own_packed = jnp.where(from_here[:, None], packed[own_tile], received)
    own_block = own_packed[:, :block_width].reshape(
        per_owner, ocean_local + atmos_local, SIDE * SIDE
    )
    own_rims = own_packed[:, block_width:].reshape(per_owner, 4, ocean_local, SIDE)
    own_state = own_block[:, :ocean_local]
    ocean_next = ocean_layer(
        pad_tile(own_state, own_rims),
        own_block[:, ocean_local:],
        own_state,
        ocean_weight,
        couple_weight,
    )
    return (atmos_next, ocean_next)


MESH = pl.DeviceIdType.MESH
PIX = SIDE * SIDE
BF = jnp.bfloat16
F32 = jnp.float32


def edge_matrix():
    out = np.zeros((2, PIX, 128), np.float32)
    for half in range(2):
        for q in range(SIDE):
            pixels = (q, q * SIDE + SIDE - 1, (SIDE - 1) * SIDE + q, q * SIDE)
            for edge, pixel in enumerate(pixels):
                out[half, pixel, half * 64 + edge * SIDE + q] = 1
    return out


def shift_matrix():
    out = np.zeros((9, PIX + 128, PIX), np.float32)
    for tap in range(9):
        for i in range(SIDE):
            for j in range(SIDE):
                row, col = i + tap // 3 - 1, j + tap % 3 - 1
                in_row, in_col = 0 <= row < SIDE, 0 <= col < SIDE
                if in_row and in_col:
                    out[tap, row * SIDE + col, i * SIDE + j] = 1
                elif in_row or in_col:
                    if in_col:
                        place = (0 if row < 0 else 2) * SIDE + col
                    else:
                        place = (3 if col < 0 else 1) * SIDE + row
                    for half in range(2):
                        out[tap, PIX + half * 64 + place, i * SIDE + j] = 1
    return out


def gelu(v):
    return 0.5 * v * (1.0 + jnp.tanh(np.float32(np.sqrt(2.0 / np.pi)) * (v + 0.044715 * (v * v * v))))


def dot(x, y):
    return jnp.dot(x, y, preferred_element_type=F32)


def owner_kernel(
    groups, nchan, at_hbm, oc_hbm, wa_hbm, wo_hbm, wc_hbm, code_s, ev_hbm, sh_hbm,
    outa, outo,
    at_v, oc_v, ev, sh, xx, ew, rl, rg, sel, wa, wo, wc, xs, an, on, og, oacc,
    loc, ssem, rsem,
):
    per_dev, ach, _ = at_hbm.shape
    och = oc_hbm.shape[1]
    atot, otot = ach * nchan, och * nchan
    tp = per_dev // nchan
    rows = ach + och
    b = lax.axis_index("tiles")
    c = lax.axis_index("chan")
    par = lax.rem(b, 2)
    sib = b + 1 - 2 * par
    nxt = lax.rem(b + 1, groups)
    prv = lax.rem(b + groups - 1, groups)
    other = jnp.where(par == 0, prv, nxt)
    half_o = och // 2

    bar = pltpu.get_barrier_semaphore()
    for d in range(nchan):
        peer = lax.rem(c + d, nchan)
        if d:
            pl.semaphore_signal(bar, inc=1, device_id=(b, peer), device_id_type=MESH)
        pl.semaphore_signal(bar, inc=1, device_id=(sib, peer), device_id_type=MESH)
    pl.semaphore_signal(bar, inc=1, device_id=(other, c), device_id_type=MESH)

    def arow(i):
        return pl.ds(pl.multiple_of(i * ach, 16), ach)

    def orow(i):
        return pl.ds(pl.multiple_of(i * och, 16), och)

    def xorow(i):
        return pl.ds(pl.multiple_of(atot + i * och, 16), och)

    def ohalf(i, k):
        return pl.ds(pl.multiple_of(i * och + k * half_o, 16), half_o)

    own = pl.ds(c * tp, tp)
    locals_ = [
        (at_hbm, at_v),
        (oc_hbm, oc_v),
        (ev_hbm, ev),
        (at_hbm.at[own], xx.at[:, arow(c), :]),
        (oc_hbm.at[own], xx.at[:, xorow(c), :]),
        (sh_hbm, sh),
        (wa_hbm, wa.at[:, arow(c), :]),
        (wo_hbm, wo.at[:, orow(c), :]),
        (wc_hbm, wc.at[orow(c), :]),
    ]
    lcopies = [pltpu.make_async_copy(s, t, loc.at[i]) for i, (s, t) in enumerate(locals_)]
    for cp in lcopies:
        cp.start()
    for cp in lcopies[:3]:
        cp.wait()

    masks = per_dev * 4
    here = masks + par * per_dev
    lane128 = lax.broadcasted_iota(jnp.int32, (1, 128), 1)
    for u in range(per_dev // 2):
        at_e = dot(at_v[2 * u], ev[0]) + dot(at_v[2 * u + 1], ev[1])
        oc_e = dot(oc_v[2 * u], ev[0]) + dot(oc_v[2 * u + 1], ev[1])
        keep = jnp.where(lane128 < 64, code_s[here + 2 * u], code_s[here + 2 * u + 1])
        ew[1, :ach, u * 128 : u * 128 + 128] = at_e.astype(BF)
        ew[1, ach:, u * 128 : u * 128 + 128] = jnp.where(keep > 0, oc_e, 0.0).astype(BF)

    counter = [0]

    def remote(src, dst, dev):
        i = counter[0]
        counter[0] += 1
        return pltpu.make_async_remote_copy(
            src_ref=src, dst_ref=dst, send_sem=ssem.at[i], recv_sem=rsem.at[i],
            device_id=dev, device_id_type=MESH,
        )

    pl.semaphore_wait(bar, 2 * nchan)
    edges = [remote(ew.at[1], ew.at[0], (nxt, c)), remote(ew.at[1], ew.at[2], (prv, c))]
    for cp in edges:
        cp.start()
    states, weights = [], []
    for d in range(1, nchan):
        peer = lax.rem(c + d, nchan)
        theirs = pl.ds(peer * tp, tp)
        states += [
            remote(at_v.at[theirs], xx.at[:, arow(c), :], (b, peer)),
            remote(oc_v.at[theirs], xx.at[:, xorow(c), :], (b, peer)),
        ]
    for cp in states:
        cp.start()
    for cp in lcopies[6:]:
        cp.wait()
    taps = pl.ds(par * 4, 5)
    big_weights = []
    for d in range(1, nchan):
        peer = lax.rem(c + d, nchan)
        weights += [
            remote(wo.at[:, ohalf(c, par), :], wo.at[:, ohalf(c, par), :], (b, peer)),
            remote(wc.at[ohalf(c, par), :], wc.at[ohalf(c, par), :], (b, peer)),
        ]
        big_weights.append(remote(wa.at[taps, arow(c), :], wa.at[taps, arow(c), :], (b, peer)))
    for cp in weights:
        cp.start()

    width = per_dev * 64
    lane = lax.broadcasted_iota(jnp.int32, (1, width), 1)
    strip, place = lane // SIDE, lane % SIDE
    src = jnp.zeros((1, width), jnp.int32)
    for t in range(per_dev):
        for s in range(4):
            code = code_s[s * per_dev + t]
            turn = code & 7
            back = jnp.where(turn >= 4, SIDE - 1, 0)
            step = jnp.where(turn >= 4, -1, 1)
            base = (code >> 3) * 64 + (turn & 3) * SIDE
            src = jnp.where(strip == t * 4 + s, base + back + step * place, src)

    row_ids = lax.broadcasted_iota(jnp.int32, (128, width), 0)

    @pl.loop(0, 3 * width // 128)
    def _(k):
        hit = (row_ids + k * 128) == src
        sel[pl.ds(pl.multiple_of(k * 128, 128), 128), :] = jnp.where(hit, 1.0, 0.0).astype(BF)

    nrows = outo.shape[0]
    picks = [jnp.int32(0)] * nrows
    rank = jnp.int32(0)
    own_rank = jnp.int32(0)
    for n in range(2 * per_dev):
        sea = code_s[masks + n]
        for i in range(nrows):
            picks[i] = jnp.where((sea == 1) & (rank == 2 * i + par), n, picks[i])
        own_rank = jnp.where(n == par * per_dev + c * tp, rank, own_rank)
        rank = rank + sea
    own_sea = code_s[here + c * tp] == 1
    takes_first = [own_sea & (own_rank % 2 == p) for p in range(2)]

    for cp in edges:
        cp.wait_recv()
    rim = dot(ew[0], sel[:width]) + dot(ew[1], sel[width : 2 * width]) + dot(ew[2], sel[2 * width :])
    rim = rim.astype(BF)
    for i in range(nchan):
        rl[i] = rim[:, i * 128 : i * 128 + 128]
    rims = []
    for d in range(1, nchan):
        peer = lax.rem(c + d, nchan)
        rims.append(remote(rl.at[peer], rg.at[c], (b, peer)))
    for cp in rims + big_weights:
        cp.start()
    own_rim = pltpu.make_async_copy(rl.at[c], rg.at[c], loc.at[9])
    own_rim.start()

    forwards = []
    for d in range(1, nchan):
        origin = lax.rem(c + nchan - d, nchan)
        forwards += [
            remote(wo.at[:, ohalf(origin, par), :], wo.at[:, ohalf(origin, par), :], (sib, c)),
            remote(wc.at[ohalf(origin, par), :], wc.at[ohalf(origin, par), :], (sib, c)),
        ]
    for got, fwd in zip(weights, forwards):
        got.wait_recv()
        fwd.start()
    for cp in lcopies[3:6]:
        cp.wait()
    for cp in states:
        cp.wait_recv()
    own_rim.wait()
    for cp in rims:
        cp.wait_recv()

    ring = jnp.concatenate(
        [rg[i, :ach] for i in range(nchan)] + [rg[i, ach:] for i in range(nchan)], axis=0
    )
    parts = []
    for j in range(tp):
        mine = jnp.where(lane128 // 64 == j, ring, jnp.zeros_like(ring))
        parts.append(jnp.concatenate([xx[j], mine], axis=1))

    def shift(tap):
        for j in range(tp):
            xs[tap, :, j * PIX : (j + 1) * PIX] = dot(parts[j], sh[tap]).astype(BF)

    pl.loop(0, 4)(shift)
    pl.loop(5, 9)(shift)

    def taken(tap, lo, hi, j):
        return xx[j, lo:hi] if tap == 4 else xs[tap, lo:hi, j * PIX : (j + 1) * PIX]

    for cp in forwards:
        cp.wait_recv()
    for j in range(tp):
        acc = jnp.zeros((otot, PIX), F32)
        for tap in range(9):
            acc = acc + dot(wo[tap], taken(tap, atot, atot + otot, j))
        oacc[j] = acc

    big_forwards = []
    for d in range(1, nchan):
        origin = lax.rem(c + nchan - d, nchan)
        ftaps = pl.ds(par * 5, 4)
        fwd = remote(wa.at[ftaps, arow(origin), :], wa.at[ftaps, arow(origin), :], (sib, c))
        big_weights[d - 1].wait_recv()
        fwd.start()
        big_forwards.append(fwd)
    for cp in big_forwards:
        cp.wait_recv()

    dest = pl.ds(c * tp, tp)
    finals = []
    for j in range(tp):
        acc = jnp.zeros((atot, PIX), F32)
        for tap in range(9):
            acc = acc + dot(wa[tap], taken(tap, 0, atot, j))
        an[j] = (xx[j, :atot].astype(F32) + gelu(acc)).astype(BF)
    for d in range(1, nchan):
        peer = lax.rem(c + d, nchan)
        cp = remote(an.at[:, arow(peer), :], outa.at[dest], (b, peer))
        cp.start()
        finals.append(cp)
    own_a = pltpu.make_async_copy(an.at[:, arow(c), :], outa.at[dest], loc.at[10])
    own_a.start()
    fresh = []
    for j in range(tp):
        acc = oacc[j] + dot(wc[...], an[j])
        fresh.append((xx[j, atot:].astype(F32) + gelu(acc)).astype(BF))
    for p in range(2):
        on[p] = jnp.where(takes_first[p], fresh[0], fresh[1])
    slot = par * nchan + c
    for d in range(nchan):
        peer = lax.rem(c + d, nchan)
        for block, p in ((b, par), (sib, 1 - par)) if d else ((sib, 1 - par),):
            cp = remote(on.at[p, orow(peer), :], og.at[slot], (block, peer))
            cp.start()
            finals.append(cp)
    own_o = pltpu.make_async_copy(on.at[par, orow(c), :], og.at[slot], loc.at[11])
    own_o.start()
    own_a.wait()
    own_o.wait()
    for cp in finals:
        cp.wait_recv()
    for i in range(nrows):
        outo[i] = og[picks[i] >> 1]
    for cp in edges + states + weights + big_weights + rims + forwards + big_forwards + finals:
        cp.wait_send()


def local_owner(
    atmos_state, ocean_state, atmos_weight, ocean_weight, couple_weight, sea_mask, neighbours, rotations
):
    groups, nchan = lax.axis_size("tiles"), lax.axis_size("chan")
    per_dev, ach, _ = atmos_state.shape
    och = ocean_state.shape[1]
    atot, otot, tp = ach * nchan, och * nchan, per_dev // nchan
    rows, width = ach + och, per_dev * 64
    copies = 2 + 11 * (nchan - 1) + 10 * (nchan - 1) + nchan + 6
    group = lax.axis_index("tiles")
    adjacent = lax.dynamic_slice_in_dim(neighbours, group * per_dev, per_dev, 0)
    turns = lax.dynamic_slice_in_dim(rotations, group * per_dev, per_dev, 0)
    near = (adjacent // per_dev - group + 1) % groups * per_dev + adjacent % per_dev
    pair_mask = lax.dynamic_slice_in_dim(sea_mask, group // 2 * 2 * per_dev, 2 * per_dev, 0)
    codes = jnp.concatenate([(near * 8 + turns).T.reshape(per_dev * 4), pair_mask])
    anyspace = pl.BlockSpec(memory_space=pl.ANY)
    smem = pl.BlockSpec(memory_space=pltpu.SMEM)
    return pl.pallas_call(
        functools.partial(owner_kernel, groups, nchan),
        out_shape=(
            jax.ShapeDtypeStruct(atmos_state.shape, BF),
            jax.ShapeDtypeStruct((per_dev * 3 // 4, och, PIX), BF),
        ),
        in_specs=[anyspace] * 5 + [smem] + [anyspace] * 2,
        out_specs=(anyspace, pl.BlockSpec(memory_space=pltpu.VMEM)),
        scratch_shapes=[
            pltpu.VMEM((per_dev, ach, PIX), BF),
            pltpu.VMEM((per_dev, och, PIX), BF),
            pltpu.VMEM((2, PIX, 128), BF),
            pltpu.VMEM((9, PIX + 128, PIX), BF),
            pltpu.VMEM((tp, atot + otot, PIX), BF),
            pltpu.VMEM((3, rows, width), BF),
            pltpu.VMEM((nchan, rows, 128), BF),
            pltpu.VMEM((nchan, rows, 128), BF),
            pltpu.VMEM((3 * width, width), BF),
            pltpu.VMEM((9, atot, atot), BF),
            pltpu.VMEM((9, otot, otot), BF),
            pltpu.VMEM((otot, atot), BF),
            pltpu.VMEM((9, atot + otot, tp * PIX), BF),
            pltpu.VMEM((tp, atot, PIX), BF),
            pltpu.VMEM((tp, otot, PIX), BF),
            pltpu.VMEM((2 * nchan, och, PIX), BF),
            pltpu.VMEM((tp, otot, PIX), F32),
            pltpu.SemaphoreType.DMA((12,)),
            pltpu.SemaphoreType.DMA((copies,)),
            pltpu.SemaphoreType.DMA((copies,)),
        ],
        compiler_params=pltpu.CompilerParams(
            collective_id=0, has_side_effects=True, vmem_limit_bytes=62 * 2**20
        ),
        cost_estimate=pl.CostEstimate(flops=2 * 10**9, bytes_accessed=4 * 10**6, transcendentals=170000),
    )(
        atmos_state, ocean_state, atmos_weight, ocean_weight, couple_weight, codes,
        jnp.asarray(edge_matrix(), BF), jnp.asarray(shift_matrix(), BF),
    )


def solution(mesh):
    body = local_owner if mesh.shape["chan"] == 4 else local
    placed = (
        P("tiles", "chan", None),
        P("tiles", "chan", None),
        P(None, "chan", None),
        P(None, "chan", None),
        P("chan", None),
        P(),
        P(),
        P(),
    )
    return jax.shard_map(
        body,
        mesh=mesh,
        in_specs=placed,
        out_specs=(P("tiles", "chan", None), P("tiles", "chan", None)),
        check_vma=False,
    )
```

```python
import functools

import jax
import jax.numpy as jnp
import numpy as np
from jax import lax
from jax.experimental import pallas as pl
from jax.experimental.pallas import tpu as pltpu
from jax.sharding import PartitionSpec as P

SIDE = 16


def padded_2(cells, sides, width):
    for axis, dim in sides:
        count = lax.axis_size(axis)
        head = lax.slice_in_dim(cells, 0, width, axis=dim)
        tail = lax.slice_in_dim(cells, cells.shape[dim] - width, cells.shape[dim], axis=dim)
        cells = jnp.concatenate(
            [
                lax.ppermute(tail, axis, [(i, (i + 1) % count) for i in range(count)]),
                cells,
                lax.ppermute(head, axis, [((i + 1) % count, i) for i in range(count)]),
            ],
            axis=dim,
        )
    return cells


def partner(value, axis, distance):
    mask = 2**distance
    pairs = [(source, source ^ mask) for source in range(lax.axis_size(axis))]
    return lax.ppermute(value, axis, pairs)


def edge_set(tile_field):
    tile_count, chan_count = (tile_field.shape[0], tile_field.shape[1])
    tile_grid = tile_field.reshape(tile_count, chan_count, SIDE, SIDE)
    return jnp.stack(
        [
            tile_grid[:, :, 0, :],
            tile_grid[:, :, :, SIDE - 1],
            tile_grid[:, :, SIDE - 1, :],
            tile_grid[:, :, :, 0],
        ],
        axis=2,
    )


def pick_rims(edge_strips, adjacent, turn_codes):
    picked = edge_strips[adjacent]
    side_index = turn_codes % 4
    chosen = picked[:, :, :, 0, :]
    for edge_id in range(1, 4):
        chosen = jnp.where(
            (side_index == edge_id)[:, :, None, None], picked[:, :, :, edge_id, :], chosen
        )
    return jnp.where((turn_codes >= 4)[:, :, None, None], chosen[..., ::-1], chosen)


def pad_tile(tile_field, rim_cells):
    tile_count, chan_count = (tile_field.shape[0], tile_field.shape[1])
    tile_grid = tile_field.reshape(tile_count, chan_count, SIDE, SIDE)
    upper_row = jnp.pad(rim_cells[:, 0], ((0, 0), (0, 0), (1, 1)))[:, :, None, :]
    bottom = jnp.pad(rim_cells[:, 2], ((0, 0), (0, 0), (1, 1)))[:, :, None, :]
    middle = jnp.concatenate(
        [rim_cells[:, 3][:, :, :, None], tile_grid, rim_cells[:, 1][:, :, :, None]], axis=3
    )
    assembled = jnp.concatenate([upper_row, middle, bottom], axis=2).reshape(
        tile_count, chan_count, (SIDE + 2) * (SIDE + 2)
    )
    return jnp.pad(assembled, ((0, 0), (0, 0), (0, 2)))


def trim_columns(accum):
    tile_count, chan_count = (accum.shape[0], accum.shape[1])
    return accum.reshape(tile_count, chan_count, SIDE, SIDE + 2)[:, :, :, :SIDE].reshape(
        tile_count, chan_count, SIDE * SIDE
    )


def conv_step(weight, accum, piece):
    row_width = SIDE + 2
    out_span = SIDE * row_width
    for tap_index in range(9):
        offset = tap_index // 3 * row_width + tap_index % 3
        accum = accum + jnp.einsum(
            "oc,bcp->bop",
            weight[tap_index],
            piece[:, :, offset : offset + out_span],
            preferred_element_type=jnp.float32,
        )
    return accum


def ocean_layer(padded, forcing, own_state, ocean_weight, couple_weight):
    tile_count = padded.shape[0]
    out_chans = ocean_weight.shape[1]
    conv_start = jnp.zeros((tile_count, out_chans, SIDE * (SIDE + 2)), jnp.float32)
    conv_accum = conv_step(
        ocean_weight, conv_start, lax.all_gather(padded, "chan", axis=1, tiled=True)
    )
    couple_accum = jnp.einsum(
        "oc,bcp->bop",
        couple_weight,
        lax.all_gather(forcing, "chan", axis=1, tiled=True),
        preferred_element_type=jnp.float32,
    )
    mixed = trim_columns(conv_accum) + couple_accum
    return (own_state.astype(jnp.float32) + jax.nn.gelu(mixed, approximate=True)).astype(
        jnp.bfloat16
    )


def local(
    atmos_state,
    ocean_state,
    atmos_weight,
    ocean_weight,
    couple_weight,
    sea_mask,
    neighbours,
    rotations,
):
    per_dev = atmos_state.shape[0]
    atmos_local = atmos_state.shape[1]
    ocean_local = ocean_state.shape[1]
    groups = lax.axis_size("tiles")
    tile_group = lax.axis_index("tiles")
    first_tile = tile_group * per_dev
    sea_here = lax.dynamic_slice_in_dim(sea_mask, first_tile, per_dev, 0)
    sea_field = ocean_state * sea_here.astype(jnp.bfloat16)[:, None, None]
    edge_strips = jnp.concatenate([edge_set(atmos_state), edge_set(sea_field)], axis=1)
    widened = padded_2(edge_strips.reshape(per_dev, -1), (("tiles", 0),), per_dev)
    widened = widened.reshape(3 * per_dev, atmos_local + ocean_local, 4, SIDE)
    adjacent = lax.dynamic_slice_in_dim(neighbours, first_tile, per_dev, 0)
    turn_codes = lax.dynamic_slice_in_dim(rotations, first_tile, per_dev, 0)
    local_adjacent = (adjacent // per_dev - tile_group + 1) % groups * per_dev + adjacent % per_dev
    rim_cells = pick_rims(widened, local_adjacent, turn_codes)
    atmos_pad = pad_tile(atmos_state, rim_cells[:, :, :atmos_local])
    atmos_start = jnp.zeros((per_dev, atmos_weight.shape[1], SIDE * (SIDE + 2)), jnp.float32)
    atmos_accum = conv_step(
        atmos_weight, atmos_start, lax.all_gather(atmos_pad, "chan", axis=1, tiled=True)
    )
    atmos_next = (
        atmos_state.astype(jnp.float32) + jax.nn.gelu(trim_columns(atmos_accum), approximate=True)
    ).astype(jnp.bfloat16)
    per_owner = per_dev * 3 // 4
    ocean_total = per_owner * groups
    counts = jnp.sum(sea_mask.reshape(groups, per_dev), axis=1)
    starts = jnp.cumsum(counts) - counts
    sea_rank = jnp.cumsum(sea_mask) - 1
    rank_spots = jnp.where(sea_mask == 1, sea_rank, ocean_total)
    tile_of_rank = (
        jnp.zeros((ocean_total,), jnp.int32)
        .at[rank_spots]
        .set(jnp.arange(sea_mask.shape[0], dtype=jnp.int32), mode="drop")
    )
    my_first = starts[tile_group]
    my_last = my_first + counts[tile_group]
    parity = tile_group % 2
    pair_base = tile_group // 2 * 2 * per_owner
    slot_ids = jnp.arange(per_owner, dtype=jnp.int32)
    ranks_send = pair_base + 2 * slot_ids + (1 - parity)
    ranks_own = pair_base + 2 * slot_ids + parity
    send_tile = jnp.clip(tile_of_rank[ranks_send] - first_tile, 0, per_dev - 1)
    own_tile = jnp.clip(tile_of_rank[ranks_own] - first_tile, 0, per_dev - 1)
    from_here = (ranks_own >= my_first) & (ranks_own < my_last)
    block_width = (ocean_local + atmos_local) * SIDE * SIDE
    sea_block = jnp.concatenate([ocean_state, atmos_next], axis=1).reshape(per_dev, block_width)
    rim_flat = rim_cells[:, :, atmos_local:].reshape(per_dev, -1)
    packed = jnp.concatenate([sea_block, rim_flat], axis=1)
    received = partner(packed[send_tile], "tiles", 0)
    own_packed = jnp.where(from_here[:, None], packed[own_tile], received)
    own_block = own_packed[:, :block_width].reshape(
        per_owner, ocean_local + atmos_local, SIDE * SIDE
    )
    own_rims = own_packed[:, block_width:].reshape(per_owner, 4, ocean_local, SIDE)
    own_state = own_block[:, :ocean_local]
    ocean_next = ocean_layer(
        pad_tile(own_state, own_rims),
        own_block[:, ocean_local:],
        own_state,
        ocean_weight,
        couple_weight,
    )
    return (atmos_next, ocean_next)


MESH = pl.DeviceIdType.MESH
PIX = SIDE * SIDE
BF = jnp.bfloat16
F32 = jnp.float32


def edge_matrix():
    out = np.zeros((2, PIX, 128), np.float32)
    for half in range(2):
        for q in range(SIDE):
            pixels = (q, q * SIDE + SIDE - 1, (SIDE - 1) * SIDE + q, q * SIDE)
            for edge, pixel in enumerate(pixels):
                out[half, pixel, half * 64 + edge * SIDE + q] = 1
    return out


def shift_matrix():
    out = np.zeros((9, PIX + 128, PIX), np.float32)
    for tap in range(9):
        for i in range(SIDE):
            for j in range(SIDE):
                row, col = i + tap // 3 - 1, j + tap % 3 - 1
                in_row, in_col = 0 <= row < SIDE, 0 <= col < SIDE
                if in_row and in_col:
                    out[tap, row * SIDE + col, i * SIDE + j] = 1
                elif in_row or in_col:
                    if in_col:
                        place = (0 if row < 0 else 2) * SIDE + col
                    else:
                        place = (3 if col < 0 else 1) * SIDE + row
                    for half in range(2):
                        out[tap, PIX + half * 64 + place, i * SIDE + j] = 1
    return out


BLOCKS = (
    [(t, None) for t in range(4)] + [(None, (0, 1)), (None, (2, 3)), (8, None)]
    + [(t, None) for t in range(4, 8)] + [(None, (4, 5)), (None, (6, 7)), (None, (8, 8))]
)


def gelu(v):
    return 0.5 * v * (1.0 + jnp.tanh(np.float32(np.sqrt(2.0 / np.pi)) * (v + 0.044715 * (v * v * v))))


def dot(x, y):
    return jnp.dot(x, y, preferred_element_type=F32)


def owner_kernel(
    groups, nchan, at_hbm, oc_hbm, wa_hbm, wo_hbm, wc_hbm, mask_hbm, nbr_hbm, rot_hbm, ev_hbm, sh_hbm,
    outa, outo,
    at_v, oc_v, ev, sh, xx, ew, rl, rg, sel, wa, wo, wc, xs, an, on, og, oacc, wn, mask_s, nbr_s, rot_s,
    loc, ssem, rsem,
):
    per_dev, ach, _ = at_hbm.shape
    och = oc_hbm.shape[1]
    atot, otot = ach * nchan, och * nchan
    tp = per_dev // nchan
    rows = ach + och
    b = lax.axis_index("tiles")
    c = lax.axis_index("chan")
    par = lax.rem(b, 2)
    sib = b + 1 - 2 * par
    nxt = lax.rem(b + 1, groups)
    prv = lax.rem(b + groups - 1, groups)
    other = jnp.where(par == 0, prv, nxt)
    half_o = och // 2

    bar = pltpu.get_barrier_semaphore()
    for d in range(nchan):
        peer = lax.rem(c + d, nchan)
        if d:
            pl.semaphore_signal(bar, inc=1, device_id=(b, peer), device_id_type=MESH)
        pl.semaphore_signal(bar, inc=1, device_id=(sib, peer), device_id_type=MESH)
    pl.semaphore_signal(bar, inc=1, device_id=(other, c), device_id_type=MESH)

    def arow(i):
        return pl.ds(pl.multiple_of(i * ach, 16), ach)

    def orow(i):
        return pl.ds(pl.multiple_of(i * och, 16), och)

    def xorow(i):
        return pl.ds(pl.multiple_of(atot + i * och, 16), och)

    def ohalf(i, k):
        return pl.ds(pl.multiple_of(i * och + k * half_o, 16), half_o)

    own = pl.ds(c * tp, tp)
    locals_ = [
        (at_hbm, at_v),
        (oc_hbm, oc_v),
        (ev_hbm, ev),
        (at_hbm.at[own], xx.at[:, arow(c), :]),
        (oc_hbm.at[own], xx.at[:, xorow(c), :]),
        (sh_hbm, sh),
        (wa_hbm, wn),
        (wo_hbm, wo.at[:, orow(c), :]),
        (wc_hbm, wc.at[orow(c), :]),
        (mask_hbm, mask_s),
        (nbr_hbm, nbr_s),
        (rot_hbm, rot_s),
    ]
    lcopies = [pltpu.make_async_copy(s, t, loc.at[i]) for i, (s, t) in enumerate(locals_)]
    for cp in lcopies:
        cp.start()
    for cp in lcopies[:3] + lcopies[9:]:
        cp.wait()

    first = b * per_dev
    pair_first = (b - par) * per_dev
    lane128 = lax.broadcasted_iota(jnp.int32, (1, 128), 1)
    for u in range(per_dev // 2):
        at_e = dot(at_v[2 * u], ev[0]) + dot(at_v[2 * u + 1], ev[1])
        oc_e = dot(oc_v[2 * u], ev[0]) + dot(oc_v[2 * u + 1], ev[1])
        keep = jnp.where(lane128 < 64, mask_s[first + 2 * u], mask_s[first + 2 * u + 1])
        ew[1, :ach, u * 128 : u * 128 + 128] = at_e.astype(BF)
        ew[1, ach:, u * 128 : u * 128 + 128] = jnp.where(keep > 0, oc_e, 0.0).astype(BF)

    counter = [0]

    def remote(src, dst, dev):
        i = counter[0]
        counter[0] += 1
        return pltpu.make_async_remote_copy(
            src_ref=src, dst_ref=dst, send_sem=ssem.at[i], recv_sem=rsem.at[i],
            device_id=dev, device_id_type=MESH,
        )

    pl.semaphore_wait(bar, 2 * nchan)
    edges = [remote(ew.at[1], ew.at[0], (nxt, c)), remote(ew.at[1], ew.at[2], (prv, c))]
    for cp in edges:
        cp.start()
    states, weights = [], []
    for d in range(1, nchan):
        peer = lax.rem(c + d, nchan)
        theirs = pl.ds(peer * tp, tp)
        states += [
            remote(at_v.at[theirs], xx.at[:, arow(c), :], (b, peer)),
            remote(oc_v.at[theirs], xx.at[:, xorow(c), :], (b, peer)),
        ]
    for cp in states:
        cp.start()
    for cp in lcopies[6:9]:
        cp.wait()
    for i, (lo, hi) in enumerate(BLOCKS):
        if lo is not None:
            block = wn[lo, :, :128]
        else:
            block = jnp.concatenate([wn[hi[0], :, 128:], wn[hi[1], :, 128:]], axis=1)
        wa[i, arow(c), :] = block
    taps = pl.ds(par * 7, 7)
    big_weights = []
    for d in range(1, nchan):
        peer = lax.rem(c + d, nchan)
        weights += [
            remote(wo.at[:, ohalf(c, par), :], wo.at[:, ohalf(c, par), :], (b, peer)),
            remote(wc.at[ohalf(c, par), :], wc.at[ohalf(c, par), :], (b, peer)),
        ]
        big_weights.append(remote(wa.at[taps, arow(c), :], wa.at[taps, arow(c), :], (b, peer)))
    for cp in weights:
        cp.start()

    width = per_dev * 64
    lane = lax.broadcasted_iota(jnp.int32, (1, width), 1)
    strip, place = lane // SIDE, lane % SIDE
    src = jnp.zeros((1, width), jnp.int32)
    for t in range(per_dev):
        for s in range(4):
            near, turn = nbr_s[s, first + t], rot_s[s, first + t] & 7
            slot = near // per_dev - b + 1
            slot = jnp.where(slot < 0, slot + groups, jnp.where(slot >= groups, slot - groups, slot))
            back = jnp.where(turn >= 4, SIDE - 1, 0)
            step = jnp.where(turn >= 4, -1, 1)
            base = slot * width + near % per_dev * 64 + (turn & 3) * SIDE
            src = jnp.where(strip == t * 4 + s, base + back + step * place, src)

    row_ids = lax.broadcasted_iota(jnp.int32, (128, width), 0)

    @pl.loop(0, 3 * width // 128)
    def _(k):
        hit = (row_ids + k * 128) == src
        sel[pl.ds(pl.multiple_of(k * 128, 128), 128), :] = jnp.where(hit, 1.0, 0.0).astype(BF)

    nrows = outo.shape[0]
    picks = [jnp.int32(0)] * nrows
    rank = jnp.int32(0)
    own_rank = jnp.int32(0)
    for n in range(2 * per_dev):
        sea = mask_s[pair_first + n]
        for i in range(nrows):
            picks[i] = jnp.where((sea == 1) & (rank == 2 * i + par), n, picks[i])
        own_rank = jnp.where(n == par * per_dev + c * tp, rank, own_rank)
        rank = rank + sea
    own_sea = mask_s[first + c * tp] == 1
    takes_first = [own_sea & (own_rank % 2 == p) for p in range(2)]

    for cp in edges:
        cp.wait_recv()
    rim = dot(ew[0], sel[:width]) + dot(ew[1], sel[width : 2 * width]) + dot(ew[2], sel[2 * width :])
    rim = rim.astype(BF)
    for i in range(nchan):
        rl[i] = rim[:, i * 128 : i * 128 + 128]
    rims = []
    for d in range(1, nchan):
        peer = lax.rem(c + d, nchan)
        rims.append(remote(rl.at[peer], rg.at[c], (b, peer)))
    for cp in rims + big_weights:
        cp.start()
    own_rim = pltpu.make_async_copy(rl.at[c], rg.at[c], loc.at[12])
    own_rim.start()

    forwards = []
    for d in range(1, nchan):
        origin = lax.rem(c + nchan - d, nchan)
        forwards += [
            remote(wo.at[:, ohalf(origin, par), :], wo.at[:, ohalf(origin, par), :], (sib, c)),
            remote(wc.at[ohalf(origin, par), :], wc.at[ohalf(origin, par), :], (sib, c)),
        ]
    for got, fwd in zip(weights, forwards):
        got.wait_recv()
        fwd.start()
    for cp in lcopies[3:6]:
        cp.wait()
    for cp in states:
        cp.wait_recv()
    own_rim.wait()
    for cp in rims:
        cp.wait_recv()

    ring = jnp.concatenate(
        [rg[i, :ach] for i in range(nchan)] + [rg[i, ach:] for i in range(nchan)], axis=0
    )
    parts = []
    for j in range(tp):
        mine = jnp.where(lane128 // 64 == j, ring, jnp.zeros_like(ring))
        parts.append(jnp.concatenate([xx[j], mine], axis=1))

    def shift(tap):
        for j in range(tp):
            xs[tap, :, j * PIX : (j + 1) * PIX] = dot(parts[j], sh[tap]).astype(BF)

    pl.loop(0, 4)(shift)
    pl.loop(5, 9)(shift)

    def taken(tap, lo, hi, j):
        return xx[j, lo:hi] if tap == 4 else xs[tap, lo:hi, j * PIX : (j + 1) * PIX]

    for cp in forwards:
        cp.wait_recv()
    for j in range(tp):
        acc = jnp.zeros((otot, PIX), F32)
        for tap in range(9):
            acc = acc + dot(wo[tap], taken(tap, atot, atot + otot, j))
        oacc[j] = acc

    def block_of(i, j):
        lo, hi = BLOCKS[i]
        if lo is not None:
            return taken(lo, 0, 128, j)
        last = taken(hi[1], 128, atot, j)
        return jnp.concatenate(
            [taken(hi[0], 128, atot, j), jnp.zeros_like(last) if hi[0] == hi[1] else last], axis=0
        )

    dest = pl.ds(c * tp, tp)
    finals = []

    def channels(owner):
        for j in range(tp):
            acc = jnp.zeros((ach, PIX), F32)
            for i in range(0, 14, 2):
                pair = jnp.concatenate([wa[i, arow(owner)], wa[i + 1, arow(owner)]], axis=1)
                acc = acc + dot(pair, jnp.concatenate([block_of(i, j), block_of(i + 1, j)], axis=0))
            an[j, arow(owner)] = (xx[j, arow(owner)].astype(F32) + gelu(acc)).astype(BF)

    channels(c)
    own_a = pltpu.make_async_copy(an.at[:, arow(c), :], outa.at[dest], loc.at[13])
    own_a.start()
    big_forwards = []

    def pass_on(d):
        origin = lax.rem(c + nchan - d, nchan)
        blocks = wa.at[taps, arow(origin), :]
        big_weights[d - 1].wait_recv()
        fwd = remote(blocks, blocks, (sib, c))
        fwd.start()
        big_forwards.append(fwd)

    pass_on(1)
    for d in range(1, nchan):
        if d + 1 < nchan:
            pass_on(d + 1)
        big_forwards[d - 1].wait_recv()
        origin = lax.rem(c + nchan - d, nchan)
        channels(origin)
        cp = remote(an.at[:, arow(origin), :], outa.at[dest], (b, origin))
        cp.start()
        finals.append(cp)
    fresh = []
    for j in range(tp):
        acc = oacc[j] + dot(wc[...], an[j])
        fresh.append((xx[j, atot:].astype(F32) + gelu(acc)).astype(BF))
    for p in range(2):
        on[p] = jnp.where(takes_first[p], fresh[0], fresh[1])
    slot = par * nchan + c
    for d in range(nchan):
        peer = lax.rem(c + d, nchan)
        for block, p in ((b, par), (sib, 1 - par)) if d else ((sib, 1 - par),):
            cp = remote(on.at[p, orow(peer), :], og.at[slot], (block, peer))
            cp.start()
            finals.append(cp)
    own_o = pltpu.make_async_copy(on.at[par, orow(c), :], og.at[slot], loc.at[14])
    own_o.start()
    own_a.wait()
    own_o.wait()
    for cp in finals:
        cp.wait_recv()
    for i in range(nrows):
        outo[i] = og[picks[i] >> 1]
    for cp in edges + states + weights + big_weights + rims + forwards + big_forwards + finals:
        cp.wait_send()


def write_kernel(a, o, out_a, out_o, sem):
    copies = [pltpu.make_async_copy(a, out_a, sem.at[0]), pltpu.make_async_copy(o, out_o, sem.at[1])]
    for cp in copies:
        cp.start()
    for cp in copies:
        cp.wait()


def local_owner(
    atmos_state, ocean_state, atmos_weight, ocean_weight, couple_weight, sea_mask, neighbours, rotations
):
    groups, nchan = lax.axis_size("tiles"), lax.axis_size("chan")
    per_dev, ach, _ = atmos_state.shape
    och = ocean_state.shape[1]
    atot, otot, tp = ach * nchan, och * nchan, per_dev // nchan
    rows, width = ach + och, per_dev * 64
    copies = 2 + 11 * (nchan - 1) + 10 * (nchan - 1) + nchan + 6
    hbm = pl.BlockSpec(memory_space=pltpu.HBM)
    vmem = pl.BlockSpec(memory_space=pltpu.VMEM)
    kept = pl.pallas_call(
        functools.partial(owner_kernel, groups, nchan),
        out_shape=(
            jax.ShapeDtypeStruct(atmos_state.shape, BF),
            jax.ShapeDtypeStruct((per_dev * 3 // 4, och, PIX), BF),
        ),
        in_specs=[hbm] * 10,
        out_specs=(hbm, vmem),
        scratch_shapes=[
            pltpu.VMEM((per_dev, ach, PIX), BF),
            pltpu.VMEM((per_dev, och, PIX), BF),
            pltpu.VMEM((2, PIX, 128), BF),
            pltpu.VMEM((9, PIX + 128, PIX), BF),
            pltpu.VMEM((tp, atot + otot, PIX), BF),
            pltpu.VMEM((3, rows, width), BF),
            pltpu.VMEM((nchan, rows, 128), BF),
            pltpu.VMEM((nchan, rows, 128), BF),
            pltpu.VMEM((3 * width, width), BF),
            pltpu.VMEM((14, atot, 128), BF),
            pltpu.VMEM((9, otot, otot), BF),
            pltpu.VMEM((otot, atot), BF),
            pltpu.VMEM((9, atot + otot, tp * PIX), BF),
            pltpu.VMEM((tp, atot, PIX), BF),
            pltpu.VMEM((tp, otot, PIX), BF),
            pltpu.VMEM((2 * nchan, och, PIX), BF),
            pltpu.VMEM((tp, otot, PIX), F32),
            pltpu.VMEM((9, ach, atot), BF),
            pltpu.SMEM(sea_mask.shape, jnp.int32),
            pltpu.SMEM(neighbours.shape[::-1], jnp.int32),
            pltpu.SMEM(rotations.shape[::-1], jnp.int32),
            pltpu.SemaphoreType.DMA((16,)),
            pltpu.SemaphoreType.DMA((copies,)),
            pltpu.SemaphoreType.DMA((copies,)),
        ],
        compiler_params=pltpu.CompilerParams(
            collective_id=0, has_side_effects=True, vmem_limit_bytes=63 * 2**20 + 2**19
        ),
        cost_estimate=pl.CostEstimate(flops=2 * 10**9, bytes_accessed=4 * 10**6, transcendentals=170000),
    )(
        atmos_state, ocean_state, atmos_weight, ocean_weight, couple_weight, sea_mask, neighbours.T, rotations.T,
        jnp.asarray(edge_matrix(), BF), jnp.asarray(shift_matrix(), BF),
    )
    anyspace = pl.BlockSpec(memory_space=pl.ANY)
    return pl.pallas_call(
        write_kernel,
        out_shape=tuple(jax.ShapeDtypeStruct(k.shape, BF) for k in kept),
        in_specs=[anyspace] * 2,
        out_specs=(hbm, hbm),
        scratch_shapes=[pltpu.SemaphoreType.DMA((2,))],
        compiler_params=pltpu.CompilerParams(vmem_limit_bytes=63 * 2**20 + 2**19),
    )(*kept)


def solution(mesh):
    body = local_owner if mesh.shape["chan"] == 4 else local
    placed = (
        P("tiles", "chan", None),
        P("tiles", "chan", None),
        P(None, "chan", None),
        P(None, "chan", None),
        P("chan", None),
        P(),
        P(),
        P(),
    )
    return jax.shard_map(
        body,
        mesh=mesh,
        in_specs=placed,
        out_specs=(P("tiles", "chan", None), P("tiles", "chan", None)),
        check_vma=False,
    )
```

```python
import functools

import jax
import jax.numpy as jnp
import numpy as np
from jax import lax
from jax.experimental import pallas as pl
from jax.experimental.pallas import tpu as pltpu
from jax.sharding import PartitionSpec as P

SIDE = 16


def padded_2(cells, sides, width):
    for axis, dim in sides:
        count = lax.axis_size(axis)
        head = lax.slice_in_dim(cells, 0, width, axis=dim)
        tail = lax.slice_in_dim(cells, cells.shape[dim] - width, cells.shape[dim], axis=dim)
        cells = jnp.concatenate(
            [
                lax.ppermute(tail, axis, [(i, (i + 1) % count) for i in range(count)]),
                cells,
                lax.ppermute(head, axis, [((i + 1) % count, i) for i in range(count)]),
            ],
            axis=dim,
        )
    return cells


def partner(value, axis, distance):
    mask = 2**distance
    pairs = [(source, source ^ mask) for source in range(lax.axis_size(axis))]
    return lax.ppermute(value, axis, pairs)


def edge_set(tile_field):
    tile_count, chan_count = (tile_field.shape[0], tile_field.shape[1])
    tile_grid = tile_field.reshape(tile_count, chan_count, SIDE, SIDE)
    return jnp.stack(
        [
            tile_grid[:, :, 0, :],
            tile_grid[:, :, :, SIDE - 1],
            tile_grid[:, :, SIDE - 1, :],
            tile_grid[:, :, :, 0],
        ],
        axis=2,
    )


def pick_rims(edge_strips, adjacent, turn_codes):
    picked = edge_strips[adjacent]
    side_index = turn_codes % 4
    chosen = picked[:, :, :, 0, :]
    for edge_id in range(1, 4):
        chosen = jnp.where(
            (side_index == edge_id)[:, :, None, None], picked[:, :, :, edge_id, :], chosen
        )
    return jnp.where((turn_codes >= 4)[:, :, None, None], chosen[..., ::-1], chosen)


def pad_tile(tile_field, rim_cells):
    tile_count, chan_count = (tile_field.shape[0], tile_field.shape[1])
    tile_grid = tile_field.reshape(tile_count, chan_count, SIDE, SIDE)
    upper_row = jnp.pad(rim_cells[:, 0], ((0, 0), (0, 0), (1, 1)))[:, :, None, :]
    bottom = jnp.pad(rim_cells[:, 2], ((0, 0), (0, 0), (1, 1)))[:, :, None, :]
    middle = jnp.concatenate(
        [rim_cells[:, 3][:, :, :, None], tile_grid, rim_cells[:, 1][:, :, :, None]], axis=3
    )
    assembled = jnp.concatenate([upper_row, middle, bottom], axis=2).reshape(
        tile_count, chan_count, (SIDE + 2) * (SIDE + 2)
    )
    return jnp.pad(assembled, ((0, 0), (0, 0), (0, 2)))


def trim_columns(accum):
    tile_count, chan_count = (accum.shape[0], accum.shape[1])
    return accum.reshape(tile_count, chan_count, SIDE, SIDE + 2)[:, :, :, :SIDE].reshape(
        tile_count, chan_count, SIDE * SIDE
    )


def conv_step(weight, accum, piece):
    row_width = SIDE + 2
    out_span = SIDE * row_width
    for tap_index in range(9):
        offset = tap_index // 3 * row_width + tap_index % 3
        accum = accum + jnp.einsum(
            "oc,bcp->bop",
            weight[tap_index],
            piece[:, :, offset : offset + out_span],
            preferred_element_type=jnp.float32,
        )
    return accum


def ocean_layer(padded, forcing, own_state, ocean_weight, couple_weight):
    tile_count = padded.shape[0]
    out_chans = ocean_weight.shape[1]
    conv_start = jnp.zeros((tile_count, out_chans, SIDE * (SIDE + 2)), jnp.float32)
    conv_accum = conv_step(
        ocean_weight, conv_start, lax.all_gather(padded, "chan", axis=1, tiled=True)
    )
    couple_accum = jnp.einsum(
        "oc,bcp->bop",
        couple_weight,
        lax.all_gather(forcing, "chan", axis=1, tiled=True),
        preferred_element_type=jnp.float32,
    )
    mixed = trim_columns(conv_accum) + couple_accum
    return (own_state.astype(jnp.float32) + jax.nn.gelu(mixed, approximate=True)).astype(
        jnp.bfloat16
    )


def local(
    atmos_state,
    ocean_state,
    atmos_weight,
    ocean_weight,
    couple_weight,
    sea_mask,
    neighbours,
    rotations,
):
    per_dev = atmos_state.shape[0]
    atmos_local = atmos_state.shape[1]
    ocean_local = ocean_state.shape[1]
    groups = lax.axis_size("tiles")
    tile_group = lax.axis_index("tiles")
    first_tile = tile_group * per_dev
    sea_here = lax.dynamic_slice_in_dim(sea_mask, first_tile, per_dev, 0)
    sea_field = ocean_state * sea_here.astype(jnp.bfloat16)[:, None, None]
    edge_strips = jnp.concatenate([edge_set(atmos_state), edge_set(sea_field)], axis=1)
    widened = padded_2(edge_strips.reshape(per_dev, -1), (("tiles", 0),), per_dev)
    widened = widened.reshape(3 * per_dev, atmos_local + ocean_local, 4, SIDE)
    adjacent = lax.dynamic_slice_in_dim(neighbours, first_tile, per_dev, 0)
    turn_codes = lax.dynamic_slice_in_dim(rotations, first_tile, per_dev, 0)
    local_adjacent = (adjacent // per_dev - tile_group + 1) % groups * per_dev + adjacent % per_dev
    rim_cells = pick_rims(widened, local_adjacent, turn_codes)
    atmos_pad = pad_tile(atmos_state, rim_cells[:, :, :atmos_local])
    atmos_start = jnp.zeros((per_dev, atmos_weight.shape[1], SIDE * (SIDE + 2)), jnp.float32)
    atmos_accum = conv_step(
        atmos_weight, atmos_start, lax.all_gather(atmos_pad, "chan", axis=1, tiled=True)
    )
    atmos_next = (
        atmos_state.astype(jnp.float32) + jax.nn.gelu(trim_columns(atmos_accum), approximate=True)
    ).astype(jnp.bfloat16)
    per_owner = per_dev * 3 // 4
    ocean_total = per_owner * groups
    counts = jnp.sum(sea_mask.reshape(groups, per_dev), axis=1)
    starts = jnp.cumsum(counts) - counts
    sea_rank = jnp.cumsum(sea_mask) - 1
    rank_spots = jnp.where(sea_mask == 1, sea_rank, ocean_total)
    tile_of_rank = (
        jnp.zeros((ocean_total,), jnp.int32)
        .at[rank_spots]
        .set(jnp.arange(sea_mask.shape[0], dtype=jnp.int32), mode="drop")
    )
    my_first = starts[tile_group]
    my_last = my_first + counts[tile_group]
    parity = tile_group % 2
    pair_base = tile_group // 2 * 2 * per_owner
    slot_ids = jnp.arange(per_owner, dtype=jnp.int32)
    ranks_send = pair_base + 2 * slot_ids + (1 - parity)
    ranks_own = pair_base + 2 * slot_ids + parity
    send_tile = jnp.clip(tile_of_rank[ranks_send] - first_tile, 0, per_dev - 1)
    own_tile = jnp.clip(tile_of_rank[ranks_own] - first_tile, 0, per_dev - 1)
    from_here = (ranks_own >= my_first) & (ranks_own < my_last)
    block_width = (ocean_local + atmos_local) * SIDE * SIDE
    sea_block = jnp.concatenate([ocean_state, atmos_next], axis=1).reshape(per_dev, block_width)
    rim_flat = rim_cells[:, :, atmos_local:].reshape(per_dev, -1)
    packed = jnp.concatenate([sea_block, rim_flat], axis=1)
    received = partner(packed[send_tile], "tiles", 0)
    own_packed = jnp.where(from_here[:, None], packed[own_tile], received)
    own_block = own_packed[:, :block_width].reshape(
        per_owner, ocean_local + atmos_local, SIDE * SIDE
    )
    own_rims = own_packed[:, block_width:].reshape(per_owner, 4, ocean_local, SIDE)
    own_state = own_block[:, :ocean_local]
    ocean_next = ocean_layer(
        pad_tile(own_state, own_rims),
        own_block[:, ocean_local:],
        own_state,
        ocean_weight,
        couple_weight,
    )
    return (atmos_next, ocean_next)


MESH = pl.DeviceIdType.MESH
PIX = SIDE * SIDE
BF = jnp.bfloat16
F32 = jnp.float32


def edge_matrix():
    out = np.zeros((2, PIX, 128), np.float32)
    for half in range(2):
        for q in range(SIDE):
            pixels = (q, q * SIDE + SIDE - 1, (SIDE - 1) * SIDE + q, q * SIDE)
            for edge, pixel in enumerate(pixels):
                out[half, pixel, half * 64 + edge * SIDE + q] = 1
    return out


def shift_matrix():
    out = np.zeros((9, PIX + 128, PIX), np.float32)
    for tap in range(9):
        for i in range(SIDE):
            for j in range(SIDE):
                row, col = i + tap // 3 - 1, j + tap % 3 - 1
                in_row, in_col = 0 <= row < SIDE, 0 <= col < SIDE
                if in_row and in_col:
                    out[tap, row * SIDE + col, i * SIDE + j] = 1
                elif in_row or in_col:
                    if in_col:
                        place = (0 if row < 0 else 2) * SIDE + col
                    else:
                        place = (3 if col < 0 else 1) * SIDE + row
                    for half in range(2):
                        out[tap, PIX + half * 64 + place, i * SIDE + j] = 1
    return out


BLOCKS = (
    [(t, None) for t in range(4)] + [(None, (0, 1)), (None, (2, 3)), (8, None)]
    + [(t, None) for t in range(4, 8)] + [(None, (4, 5)), (None, (6, 7)), (None, (8, 8))]
)


def gelu(v):
    return 0.5 * v * (1.0 + jnp.tanh(np.float32(np.sqrt(2.0 / np.pi)) * (v + 0.044715 * (v * v * v))))


def dot(x, y):
    return jnp.dot(x, y, preferred_element_type=F32)


def owner_kernel(
    groups, nchan, at_hbm, oc_hbm, wa_hbm, wo_hbm, wc_hbm, mask_hbm, nbr_hbm, rot_hbm, ev_hbm, sh_hbm,
    outa, outo,
    at_v, oc_v, ev, sh, xx, ew, rl, rg, sel, wa, wo, wc, xs, an, on, og, oacc, wn, mask_s, nbr_s, rot_s,
    loc, ssem, rsem,
):
    per_dev, ach, _ = at_hbm.shape
    och = oc_hbm.shape[1]
    atot, otot = ach * nchan, och * nchan
    tp = per_dev // nchan
    rows = ach + och
    b = lax.axis_index("tiles")
    c = lax.axis_index("chan")
    par = lax.rem(b, 2)
    sib = b + 1 - 2 * par
    nxt = lax.rem(b + 1, groups)
    prv = lax.rem(b + groups - 1, groups)
    other = jnp.where(par == 0, prv, nxt)
    half_o = och // 2

    bar = pltpu.get_barrier_semaphore()
    for d in range(nchan):
        peer = lax.rem(c + d, nchan)
        if d:
            pl.semaphore_signal(bar, inc=1, device_id=(b, peer), device_id_type=MESH)
        pl.semaphore_signal(bar, inc=1, device_id=(sib, peer), device_id_type=MESH)
    pl.semaphore_signal(bar, inc=1, device_id=(other, c), device_id_type=MESH)

    def arow(i):
        return pl.ds(pl.multiple_of(i * ach, 16), ach)

    def orow(i):
        return pl.ds(pl.multiple_of(i * och, 16), och)

    def xorow(i):
        return pl.ds(pl.multiple_of(atot + i * och, 16), och)

    def ohalf(i, k):
        return pl.ds(pl.multiple_of(i * och + k * half_o, 16), half_o)

    own = pl.ds(c * tp, tp)
    locals_ = [
        (at_hbm, at_v),
        (oc_hbm, oc_v),
        (ev_hbm, ev),
        (at_hbm.at[own], xx.at[:, arow(c), :]),
        (oc_hbm.at[own], xx.at[:, xorow(c), :]),
        (sh_hbm, sh),
        (wa_hbm, wn),
        (wo_hbm, wo.at[:, orow(c), :]),
        (wc_hbm, wc.at[orow(c), :]),
        (mask_hbm, mask_s),
        (nbr_hbm, nbr_s),
        (rot_hbm, rot_s),
    ]
    lcopies = [pltpu.make_async_copy(s, t, loc.at[i]) for i, (s, t) in enumerate(locals_)]
    for cp in lcopies:
        cp.start()
    for cp in lcopies[:3] + lcopies[9:]:
        cp.wait()

    first = b * per_dev
    pair_first = (b - par) * per_dev
    lane128 = lax.broadcasted_iota(jnp.int32, (1, 128), 1)
    for u in range(per_dev // 2):
        at_e = dot(at_v[2 * u], ev[0]) + dot(at_v[2 * u + 1], ev[1])
        oc_e = dot(oc_v[2 * u], ev[0]) + dot(oc_v[2 * u + 1], ev[1])
        keep = jnp.where(lane128 < 64, mask_s[first + 2 * u], mask_s[first + 2 * u + 1])
        ew[1, :ach, u * 128 : u * 128 + 128] = at_e.astype(BF)
        ew[1, ach:, u * 128 : u * 128 + 128] = jnp.where(keep > 0, oc_e, 0.0).astype(BF)

    counter = [0]

    def remote(src, dst, dev):
        i = counter[0]
        counter[0] += 1
        return pltpu.make_async_remote_copy(
            src_ref=src, dst_ref=dst, send_sem=ssem.at[i], recv_sem=rsem.at[i],
            device_id=dev, device_id_type=MESH,
        )

    pl.semaphore_wait(bar, 2 * nchan)
    edges = [remote(ew.at[1], ew.at[0], (nxt, c)), remote(ew.at[1], ew.at[2], (prv, c))]
    for cp in edges:
        cp.start()
    states, weights = [], []
    for d in range(1, nchan):
        peer = lax.rem(c + d, nchan)
        theirs = pl.ds(peer * tp, tp)
        states += [
            remote(at_v.at[theirs], xx.at[:, arow(c), :], (b, peer)),
            remote(oc_v.at[theirs], xx.at[:, xorow(c), :], (b, peer)),
        ]
    for cp in states:
        cp.start()
    for cp in lcopies[6:9]:
        cp.wait()
    for i, (lo, hi) in enumerate(BLOCKS):
        if lo is not None:
            block = wn[lo, :, :128]
        else:
            block = jnp.concatenate([wn[hi[0], :, 128:], wn[hi[1], :, 128:]], axis=1)
        wa[i, arow(c), :] = block
    taps = pl.ds(par * 7, 7)
    big_weights = []
    for d in range(1, nchan):
        peer = lax.rem(c + d, nchan)
        weights += [
            remote(wo.at[:, ohalf(c, par), :], wo.at[:, ohalf(c, par), :], (b, peer)),
            remote(wc.at[ohalf(c, par), :], wc.at[ohalf(c, par), :], (b, peer)),
        ]
        big_weights.append(remote(wa.at[taps, arow(c), :], wa.at[taps, arow(c), :], (b, peer)))
    for cp in weights:
        cp.start()

    width = per_dev * 64
    lane = lax.broadcasted_iota(jnp.int32, (1, width), 1)
    strip, place = lane // SIDE, lane % SIDE
    src = jnp.zeros((1, width), jnp.int32)
    for t in range(per_dev):
        for s in range(4):
            near, turn = nbr_s[s, first + t], rot_s[s, first + t] & 7
            slot = near // per_dev - b + 1
            slot = jnp.where(slot < 0, slot + groups, jnp.where(slot >= groups, slot - groups, slot))
            back = jnp.where(turn >= 4, SIDE - 1, 0)
            step = jnp.where(turn >= 4, -1, 1)
            base = slot * width + near % per_dev * 64 + (turn & 3) * SIDE
            src = jnp.where(strip == t * 4 + s, base + back + step * place, src)

    row_ids = lax.broadcasted_iota(jnp.int32, (128, width), 0)

    @pl.loop(0, 3 * width // 128)
    def _(k):
        hit = (row_ids + k * 128) == src
        sel[pl.ds(pl.multiple_of(k * 128, 128), 128), :] = jnp.where(hit, 1.0, 0.0).astype(BF)

    nrows = outo.shape[0]
    picks = [jnp.int32(0)] * nrows
    rank = jnp.int32(0)
    own_rank = jnp.int32(0)
    for n in range(2 * per_dev):
        sea = mask_s[pair_first + n]
        for i in range(nrows):
            picks[i] = jnp.where((sea == 1) & (rank == 2 * i + par), n, picks[i])
        own_rank = jnp.where(n == par * per_dev + c * tp, rank, own_rank)
        rank = rank + sea
    own_sea = mask_s[first + c * tp] == 1
    takes_first = [own_sea & (own_rank % 2 == p) for p in range(2)]

    for cp in edges:
        cp.wait_recv()
    rim = dot(ew[0], sel[:width]) + dot(ew[1], sel[width : 2 * width]) + dot(ew[2], sel[2 * width :])
    rim = rim.astype(BF)
    for i in range(nchan):
        rl[i] = rim[:, i * 128 : i * 128 + 128]
    rims = []
    for d in range(1, nchan):
        peer = lax.rem(c + d, nchan)
        rims.append(remote(rl.at[peer], rg.at[c], (b, peer)))
    for cp in rims + big_weights:
        cp.start()
    own_rim = pltpu.make_async_copy(rl.at[c], rg.at[c], loc.at[12])
    own_rim.start()

    forwards = []
    for d in range(1, nchan):
        origin = lax.rem(c + nchan - d, nchan)
        forwards += [
            remote(wo.at[:, ohalf(origin, par), :], wo.at[:, ohalf(origin, par), :], (sib, c)),
            remote(wc.at[ohalf(origin, par), :], wc.at[ohalf(origin, par), :], (sib, c)),
        ]
    for got, fwd in zip(weights, forwards):
        got.wait_recv()
        fwd.start()
    for cp in lcopies[3:6]:
        cp.wait()
    for cp in states:
        cp.wait_recv()
    own_rim.wait()
    for cp in rims:
        cp.wait_recv()

    ring = jnp.concatenate(
        [rg[i, :ach] for i in range(nchan)] + [rg[i, ach:] for i in range(nchan)], axis=0
    )
    parts = []
    for j in range(tp):
        mine = jnp.where(lane128 // 64 == j, ring, jnp.zeros_like(ring))
        parts.append(jnp.concatenate([xx[j], mine], axis=1))

    def shift(tap):
        for j in range(tp):
            xs[tap, :, j * PIX : (j + 1) * PIX] = dot(parts[j], sh[tap]).astype(BF)

    pl.loop(0, 4)(shift)
    pl.loop(5, 9)(shift)

    def taken(tap, lo, hi, j):
        return xx[j, lo:hi] if tap == 4 else xs[tap, lo:hi, j * PIX : (j + 1) * PIX]

    for cp in forwards:
        cp.wait_recv()
    for j in range(tp):
        acc = jnp.zeros((otot, PIX), F32)
        for tap in range(9):
            acc = acc + dot(wo[tap], taken(tap, atot, atot + otot, j))
        oacc[j] = acc

    def block_of(i, j):
        lo, hi = BLOCKS[i]
        if lo is not None:
            return taken(lo, 0, 128, j)
        last = taken(hi[1], 128, atot, j)
        return jnp.concatenate(
            [taken(hi[0], 128, atot, j), jnp.zeros_like(last) if hi[0] == hi[1] else last], axis=0
        )

    dest = pl.ds(c * tp, tp)
    finals = []

    def channels(owner):
        for j in range(tp):
            acc = jnp.zeros((ach, PIX), F32)
            for i in range(0, 14, 2):
                pair = jnp.concatenate([wa[i, arow(owner)], wa[i + 1, arow(owner)]], axis=1)
                acc = acc + dot(pair, jnp.concatenate([block_of(i, j), block_of(i + 1, j)], axis=0))
            an[j, arow(owner)] = (xx[j, arow(owner)].astype(F32) + gelu(acc)).astype(BF)

    channels(c)
    own_a = pltpu.make_async_copy(an.at[:, arow(c), :], outa.at[dest], loc.at[13])
    own_a.start()
    big_forwards = []

    def pass_on(d):
        origin = lax.rem(c + nchan - d, nchan)
        blocks = wa.at[taps, arow(origin), :]
        big_weights[d - 1].wait_recv()
        fwd = remote(blocks, blocks, (sib, c))
        fwd.start()
        big_forwards.append(fwd)

    pass_on(1)
    for d in range(1, nchan):
        if d + 1 < nchan:
            pass_on(d + 1)
        big_forwards[d - 1].wait_recv()
        origin = lax.rem(c + nchan - d, nchan)
        channels(origin)
        cp = remote(an.at[:, arow(origin), :], outa.at[dest], (b, origin))
        cp.start()
        finals.append(cp)
    fresh = []
    for j in range(tp):
        acc = oacc[j] + dot(wc[...], an[j])
        fresh.append((xx[j, atot:].astype(F32) + gelu(acc)).astype(BF))
    for p in range(2):
        on[p] = jnp.where(takes_first[p], fresh[0], fresh[1])
    slot = par * nchan + c
    for d in range(nchan):
        peer = lax.rem(c + d, nchan)
        for block, p in ((b, par), (sib, 1 - par)) if d else ((sib, 1 - par),):
            cp = remote(on.at[p, orow(peer), :], og.at[slot], (block, peer))
            cp.start()
            finals.append(cp)
    own_o = pltpu.make_async_copy(on.at[par, orow(c), :], og.at[slot], loc.at[14])
    own_o.start()
    own_a.wait()
    own_o.wait()
    for cp in finals:
        cp.wait_recv()
    for i in range(nrows):
        outo[i] = og[picks[i] >> 1]
    for cp in edges + states + weights + big_weights + rims + forwards + big_forwards + finals:
        cp.wait_send()


def write_kernel(a, o, out_a, out_o):
    out_a[...] = a[...]
    out_o[...] = o[...]


def local_owner(
    atmos_state, ocean_state, atmos_weight, ocean_weight, couple_weight, sea_mask, neighbours, rotations
):
    groups, nchan = lax.axis_size("tiles"), lax.axis_size("chan")
    per_dev, ach, _ = atmos_state.shape
    och = ocean_state.shape[1]
    atot, otot, tp = ach * nchan, och * nchan, per_dev // nchan
    rows, width = ach + och, per_dev * 64
    copies = 2 + 11 * (nchan - 1) + 10 * (nchan - 1) + nchan + 6
    hbm = pl.BlockSpec(memory_space=pltpu.HBM)
    vmem = pl.BlockSpec(memory_space=pltpu.VMEM)
    kept = pl.pallas_call(
        functools.partial(owner_kernel, groups, nchan),
        out_shape=(
            jax.ShapeDtypeStruct(atmos_state.shape, BF),
            jax.ShapeDtypeStruct((per_dev * 3 // 4, och, PIX), BF),
        ),
        in_specs=[hbm] * 10,
        out_specs=(hbm, vmem),
        scratch_shapes=[
            pltpu.VMEM((per_dev, ach, PIX), BF),
            pltpu.VMEM((per_dev, och, PIX), BF),
            pltpu.VMEM((2, PIX, 128), BF),
            pltpu.VMEM((9, PIX + 128, PIX), BF),
            pltpu.VMEM((tp, atot + otot, PIX), BF),
            pltpu.VMEM((3, rows, width), BF),
            pltpu.VMEM((nchan, rows, 128), BF),
            pltpu.VMEM((nchan, rows, 128), BF),
            pltpu.VMEM((3 * width, width), BF),
            pltpu.VMEM((14, atot, 128), BF),
            pltpu.VMEM((9, otot, otot), BF),
            pltpu.VMEM((otot, atot), BF),
            pltpu.VMEM((9, atot + otot, tp * PIX), BF),
            pltpu.VMEM((tp, atot, PIX), BF),
            pltpu.VMEM((tp, otot, PIX), BF),
            pltpu.VMEM((2 * nchan, och, PIX), BF),
            pltpu.VMEM((tp, otot, PIX), F32),
            pltpu.VMEM((9, ach, atot), BF),
            pltpu.SMEM(sea_mask.shape, jnp.int32),
            pltpu.SMEM(neighbours.shape[::-1], jnp.int32),
            pltpu.SMEM(rotations.shape[::-1], jnp.int32),
            pltpu.SemaphoreType.DMA((16,)),
            pltpu.SemaphoreType.DMA((copies,)),
            pltpu.SemaphoreType.DMA((copies,)),
        ],
        compiler_params=pltpu.CompilerParams(
            collective_id=0, has_side_effects=True, vmem_limit_bytes=63 * 2**20 + 2**19
        ),
        cost_estimate=pl.CostEstimate(flops=2 * 10**9, bytes_accessed=4 * 10**6, transcendentals=170000),
    )(
        atmos_state, ocean_state, atmos_weight, ocean_weight, couple_weight, sea_mask, neighbours.T, rotations.T,
        jnp.asarray(edge_matrix(), BF), jnp.asarray(shift_matrix(), BF),
    )
    return pl.pallas_call(
        write_kernel,
        out_shape=tuple(jax.ShapeDtypeStruct(k.shape, BF) for k in kept),
        in_specs=[vmem] * 2,
        out_specs=(vmem, vmem),
        compiler_params=pltpu.CompilerParams(vmem_limit_bytes=63 * 2**20 + 2**19),
    )(*kept)


def solution(mesh):
    body = local_owner if mesh.shape["chan"] == 4 else local
    placed = (
        P("tiles", "chan", None),
        P("tiles", "chan", None),
        P(None, "chan", None),
        P(None, "chan", None),
        P("chan", None),
        P(),
        P(),
        P(),
    )
    return jax.shard_map(
        body,
        mesh=mesh,
        in_specs=placed,
        out_specs=(P("tiles", "chan", None), P("tiles", "chan", None)),
        check_vma=False,
    )
```
